32 devices in a mesh: segment: 4 (over z), frame: 4 (over y, x), row: 2 (over core).
Axes of the slice: x: 2, y: 2, z: 4, core: 2. Of those that a mesh axis runs over, the one named last changes fastest.
Arguments:
- clip_tokens: bfloat16 [4, 4, 2, 2, 64, 1536], P('segment', 'frame', 'row'), may hold values from -6 to 6
- qkv_weight: bfloat16 [4, 1536, 2304], P('segment'), may hold values from -1 to 1
- out_weight: bfloat16 [4, 768, 1536], P('segment'), may hold values from -0.21875 to 0.21875
- modulation: bfloat16 [4, 8, 3, 1536], P('segment'), may hold values from -4 to 4
- domain_ids: int32 [4], P('segment'), may hold values from 0 to 7
- tile_lists: int32 [4, 2, 2, 6], P('frame', 'row'), may hold values from 0 to 9, as said below
Outputs:
- handed: bfloat16 [4, 4, 2, 2, 64, 1536], P('segment', 'frame', 'row')
The draws below stay inside these ranges and needn't reach their ends.
Inputs may be any that keep to these rules, and one draw needn't show every extreme that they name: `tile_lists`: each row names 6 different candidates, always the tile's own one, and never a tile outside the grid.
All inputs are finite; a program needn't handle non-finite values.
Results may differ from the reference program's by a relative error of at most 0.0081.
Values may be sent and summed in bfloat16 or wider, within the bound.
No kernel may reach another device: no remote copies, remote signals or barrier semaphores. Data moves between devices by JAX's collectives and lax.ppermute only.
A program may use at most 64 MiB of HBM per device.

```python
from functools import partial
import jax
import jax.numpy as jnp
from jax import lax

D = 1536
HEADS = 6
HD = 128
DOMAINS = 8
TILE = 64
COL_TILES = 2
K_ATT = 6
CLIPS = 4
FT = 4
RT = 2


def draw_clip_tokens(key, part):
    full_shape = (CLIPS, FT, RT, COL_TILES, TILE, D)
    sample = jax.random.normal(key, full_shape, jnp.float32)
    return jnp.clip(sample, -6.0, 6.0).astype(jnp.bfloat16)


def draw_qkv_weight(key, part):
    inner_width = HEADS * HD
    sample = jnp.clip(jax.random.normal(key, (CLIPS, D, 3 * inner_width), jnp.float32), -6.0, 6.0) * D ** (-0.5)
    return jnp.clip(sample, -1.0, 1.0).astype(jnp.bfloat16)


def draw_domain_ids(key, part):
    order = jax.random.permutation(jax.random.fold_in(key, 31), CLIPS).astype(jnp.int32)
    offset = jax.random.randint(jax.random.fold_in(key, 37), (CLIPS,), 0, DOMAINS * 4099, dtype=jnp.int32)
    return ((order + offset) % DOMAINS).astype(jnp.int32)


def draw_tile_lists(key, part):
    cand_count = 5 * COL_TILES
    numbers = jnp.arange(cand_count, dtype=jnp.int32)
    slot_of = numbers // COL_TILES
    column_of = numbers % COL_TILES
    frame_pos = jnp.arange(FT, dtype=jnp.int32)[:, None, None, None]
    row_pos = jnp.arange(RT, dtype=jnp.int32)[None, :, None, None]
    own_col = jnp.arange(COL_TILES, dtype=jnp.int32)[None, None, :, None]
    usable = jnp.ones((FT, RT, COL_TILES, cand_count), dtype=bool)
    usable = usable & ~((slot_of == 1) & (frame_pos == 0))
    usable = usable & ~((slot_of == 2) & (frame_pos == FT - 1))
    usable = usable & ~((slot_of == 3) & (row_pos == 0))
    usable = usable & ~((slot_of == 4) & (row_pos == RT - 1))
    itself = (slot_of == 0) & (column_of == own_col)
    ranking = jax.random.randint(key, (FT, RT, COL_TILES, cand_count), 0, 1 << 20, dtype=jnp.int32) * cand_count + numbers
    top_mark = jnp.int32((1 << 20) * cand_count + cand_count)
    marked = jnp.where(itself, top_mark, jnp.where(usable, ranking, -1 - numbers))
    marked = jnp.broadcast_to(marked, (FT, RT, COL_TILES, cand_count))
    _, chosen = lax.top_k(marked, K_ATT)
    return chosen.astype(jnp.int32)


def block_levels(stream_key, extent, split, low, largest):
    def one(dim, shards_of):
        heights = jax.random.uniform(jax.random.fold_in(jax.random.fold_in(stream_key, 6), dim), (shards_of,), jnp.float32, low / len(split), largest / len(split))
        return jnp.repeat(jnp.exp(heights), extent[dim] // shards_of).reshape((-1,) + (1,) * (len(extent) - dim - 1))

    gain = one(*split[0])
    for cut in split[1:]:
        gain = gain * one(*cut)
    return gain


def noise(own_key, dims, width, most, cuts=(), held_as=jnp.bfloat16):
    result = width * jax.random.normal(own_key, dims, jnp.float32)
    if cuts:
        result = result * block_levels(own_key, dims, cuts, -0.22, 0.18)
    return jnp.clip(result, -most, most).astype(held_as)


def setup_inputs(seed: int = 0) -> dict:
    streams_of = jax.random.split(jax.random.key(seed), 7)
    clip_tokens = draw_clip_tokens(jax.random.fold_in(streams_of[6], 71), 0)
    qkv_weight = draw_qkv_weight(jax.random.fold_in(streams_of[6], 71), 0)
    out_weight = noise(streams_of[2], (CLIPS, HEADS * HD, D), (HEADS * HD) ** -0.5, 0.21875, ((0, 4),))
    modulation = noise(streams_of[3], (CLIPS, DOMAINS, 3, D), 1.0, 4.0, ((0, 4),))
    domain_ids = draw_domain_ids(jax.random.fold_in(streams_of[6], 71), 0)
    tile_lists = draw_tile_lists(jax.random.fold_in(streams_of[6], 71), 0)
    return dict(clip_tokens=clip_tokens, qkv_weight=qkv_weight, out_weight=out_weight, modulation=modulation, domain_ids=domain_ids, tile_lists=tile_lists)


epsilon = 1e-06

def normalize(rows, modulate):
    values = rows.astype(jnp.float32)
    row_mean = lax.optimization_barrier(jnp.mean(values, axis=-1, keepdims=True))
    centered = values - row_mean
    row_var = lax.optimization_barrier(jnp.mean(centered * centered, axis=-1, keepdims=True))
    scaled = centered * lax.rsqrt(row_var + epsilon)
    return (scaled * (1.0 + modulate[1]) + modulate[0]).astype(jnp.bfloat16)

def pick_row(cand_row, chosen_row):
    return cand_row[chosen_row]

def attend_frame(operands):
    queries, candidates, chosen = operands
    picked = jax.vmap(pick_row)(candidates, chosen)
    rows_t, col_t, count_k, tile_len, double_width = picked.shape
    inner_width = double_width // 2
    key_count = count_k * tile_len
    picked = picked.reshape(rows_t, col_t, key_count, double_width)
    key_rows = picked[..., :inner_width].reshape(rows_t, col_t, key_count, HEADS, HD).astype(jnp.float32)
    value_rows = picked[..., inner_width:].reshape(rows_t, col_t, key_count, HEADS, HD).astype(jnp.float32)
    query_rows = queries.reshape(rows_t, col_t, tile_len, HEADS, HD).astype(jnp.float32)
    scores = jnp.einsum('rtqhd,rtkhd->rthqk', query_rows, key_rows) * HD ** (-0.5)
    row_peak = lax.optimization_barrier(jnp.max(scores, axis=-1, keepdims=True))
    raised = jnp.exp(scores - row_peak)
    attn_weights = (raised / lax.optimization_barrier(jnp.sum(raised, axis=-1, keepdims=True))).astype(jnp.bfloat16)
    mixed_heads = jnp.einsum('rthqk,rtkhd->rtqhd', attn_weights.astype(jnp.float32), value_rows)
    return mixed_heads.astype(jnp.bfloat16).reshape(rows_t, col_t, tile_len, inner_width)

def one_clip(tile_lists, operands):
    tokens, qkv_part, out_part, modulation_part, domain_part = operands
    frames_t, rows_t, col_t, tile_len, model_width = tokens.shape
    inner_width = HEADS * HD
    modulate = modulation_part[domain_part].astype(jnp.float32)
    own_rows = tokens.reshape(-1, model_width)
    normed = normalize(own_rows, modulate)
    projected = jnp.dot(normed, qkv_part, preferred_element_type=jnp.float32)
    queries = projected[:, :inner_width].astype(jnp.bfloat16).reshape(frames_t, rows_t, col_t, tile_len, inner_width)
    pairs = projected[:, inner_width:].astype(jnp.bfloat16).reshape(frames_t, rows_t, col_t, tile_len, 2 * inner_width)
    padded = jnp.pad(pairs, ((1, 1), (1, 1), (0, 0), (0, 0), (0, 0)))
    candidates = jnp.concatenate([padded[1:-1, 1:-1], padded[:-2, 1:-1], padded[2:, 1:-1], padded[1:-1, :-2], padded[1:-1, 2:]], axis=2)
    mixed = lax.map(attend_frame, (queries, candidates, tile_lists))
    branch = jnp.dot(mixed.reshape(-1, inner_width), out_part, preferred_element_type=jnp.float32)
    finished = own_rows.astype(jnp.float32) + modulate[2] * branch
    return finished.astype(jnp.bfloat16).reshape(tokens.shape)

def reference(clip_tokens, qkv_weight, out_weight, modulation, domain_ids, tile_lists):
    finished = lax.map(partial(one_clip, tile_lists), (clip_tokens, qkv_weight, out_weight, modulation, domain_ids))
    return jnp.roll(finished, 1, axis=0)
```

```python
import functools

import jax
import jax.numpy as jnp
from jax import lax
from jax.experimental import pallas as pl
from jax.experimental.pallas import tpu as pltpu
from jax.sharding import PartitionSpec as P

HD = 128
EPSILON = 1e-06
MASKED = -1e30
RELAYED = (2, 2, 2)
DIRECT = 2
F32 = jnp.float32
BF16 = jnp.bfloat16
VMEM = pl.BlockSpec(memory_space=pltpu.VMEM)
SMEM = pl.BlockSpec(memory_space=pltpu.SMEM)
HBM = pl.BlockSpec(memory_space=pltpu.HBM)
PARAMS = pltpu.CompilerParams(vmem_limit_bytes=32 * 1024 * 1024)


def modulate_rows(domain_ref, modulation_ref):
    table = modulation_ref[...].astype(F32)
    row = lax.broadcasted_iota(jnp.int32, table.shape, 1)
    return jnp.sum(jnp.where(row == domain_ref[0], table, 0.0), axis=1)


def normalize(rows, shift, scale):
    values = rows.astype(F32)
    centered = values - jnp.mean(values, axis=-1, keepdims=True)
    row_var = jnp.mean(centered * centered, axis=-1, keepdims=True)
    return (centered * lax.rsqrt(row_var + EPSILON) * (1.0 + scale) + shift).astype(BF16)


def normalized(refs, modulate_ref):
    shift, scale = modulate_ref[0:1, :], modulate_ref[1:2, :]
    return jnp.concatenate([normalize(r[...], shift, scale) for r in refs], axis=0)


def projected(rows, weight_ref):
    return jnp.dot(rows, weight_ref[...], preferred_element_type=F32).astype(BF16)


def own_kernel(n_other, inner, domain_ref, modulation_hbm, weight_hbm, out_weight_hbm, own_hbm, *refs):
    other_refs = refs[:n_other]
    (modulate_ref, pair_weight_ref, out_weight_ref, own_ref, q_ref, kv_ref) = refs[n_other : n_other + 6]
    kv_other_refs = refs[n_other + 6 : 2 * n_other + 6]
    modulation_ref, q_weight_ref, sems = refs[2 * n_other + 6 :]
    first = [
        pltpu.make_async_copy(modulation_hbm, modulation_ref, sems.at[4]),
        pltpu.make_async_copy(own_hbm, own_ref, sems.at[5]),
    ]
    loads = [
        pltpu.make_async_copy(weight_hbm.at[:, pl.ds(inner, inner)], pair_weight_ref.at[:, pl.ds(0, inner)], sems.at[0]),
        pltpu.make_async_copy(weight_hbm.at[:, pl.ds(2 * inner, inner)], pair_weight_ref.at[:, pl.ds(inner, inner)], sems.at[1]),
        pltpu.make_async_copy(weight_hbm.at[:, pl.ds(0, inner)], q_weight_ref, sems.at[2]),
        pltpu.make_async_copy(out_weight_hbm, out_weight_ref, sems.at[3]),
    ]
    for load in first + loads:
        load.start()
    for load in first:
        load.wait()
    modulate_ref[...] = modulate_rows(domain_ref, modulation_ref)
    rows = normalized((own_ref, *other_refs), modulate_ref)
    count = own_ref.shape[0]
    for part in range(2):
        loads[part].wait()
        cols = slice(part * inner, (part + 1) * inner)
        pairs = jnp.dot(rows, pair_weight_ref[:, cols], preferred_element_type=F32).astype(BF16)
        for i, ref in enumerate((kv_ref, *kv_other_refs)):
            ref[:, cols] = pairs[i * count : (i + 1) * count]
    loads[2].wait()
    q_ref[...] = projected(rows[:count], q_weight_ref)
    loads[3].wait()


def pairs_kernel(n_chunks, modulate_ref, weight_ref, *refs):
    chunk_refs, kv_ref = refs[:n_chunks], refs[n_chunks]
    kv_ref[...] = projected(normalized(chunk_refs, modulate_ref), weight_ref)


def picked_bits(lists_ref, tile, count, col_tiles, slots):
    bits = jnp.int32(0)
    for k in range(count):
        number = lists_ref[tile, k]
        direction = number // col_tiles
        slot = jnp.int32(0)
        for d in range(1, 5):
            slot = jnp.where(direction == d, slots[d], slot)
        bits = bits | (jnp.int32(1) << (slot * col_tiles + number % col_tiles))
    return bits


def attend_kernel(
    n_kv, n_chunks, inner, tile_len, slots_of,
    lists_ref, modulate_ref, weight_ref, out_weight_ref, own_ref, q_ref, *refs
):
    kv_refs = refs[:n_kv]
    chunk_refs = refs[n_kv : n_kv + n_chunks]
    finished_ref = refs[n_kv + n_chunks]
    own_count = own_ref.shape[0]
    col_tiles = own_count // tile_len
    pairs = [r[...] for r in kv_refs]
    if n_chunks:
        pairs.append(projected(normalized(chunk_refs, modulate_ref), weight_ref))
    pairs = jnp.concatenate(pairs, axis=0)
    key_count = pairs.shape[0]
    slots = slots_of()
    count = lists_ref.shape[1]
    position = lax.broadcasted_iota(jnp.int32, (tile_len, key_count), 1) // tile_len
    bias = jnp.concatenate(
        [
            jnp.where(
                ((picked_bits(lists_ref, t, count, col_tiles, slots) >> position) & 1) == 1,
                0.0,
                MASKED,
            )
            for t in range(col_tiles)
        ],
        axis=0,
    )
    queries = q_ref[...]
    heads = []
    for h in range(inner // HD):
        cols = slice(h * HD, (h + 1) * HD)
        keys = pairs[:, cols]
        values = pairs[:, inner + h * HD : inner + (h + 1) * HD]
        scores = lax.dot_general(
            queries[:, cols], keys, (((1,), (1,)), ((), ())), preferred_element_type=F32
        )
        scores = scores * HD ** (-0.5) + bias
        raised = jnp.exp(scores - jnp.max(scores, axis=-1, keepdims=True))
        total = jnp.sum(raised, axis=-1, keepdims=True)
        mixed = jnp.dot(raised.astype(BF16), values, preferred_element_type=F32)
        heads.append((mixed / total).astype(BF16))
    mixed_heads = jnp.concatenate(heads, axis=1)
    branch = jnp.dot(mixed_heads, out_weight_ref[...], preferred_element_type=F32)
    finished_ref[...] = (own_ref[...].astype(F32) + modulate_ref[2:3, :] * branch).astype(BF16)


def swap_perm(size):
    return [(i, i ^ 1) for i in range(size)]


def far_perm(size):
    return [(i, i + 1) for i in range(1, size - 1, 2)] + [(i + 1, i) for i in range(1, size - 1, 2)]


def relay_perm(size):
    return [(i, i + 2) for i in range(0, size - 2, 2)] + [(i, i - 2) for i in range(3, size, 2)]


def in_hbm(x):
    return pltpu.with_memory_space_constraint(x, pltpu.HBM)


def body(clip_tokens, qkv_weight, out_weight, modulation, domain_ids, tile_lists):
    col_tiles, tile_len, width = clip_tokens.shape[3:]
    own_count = col_tiles * tile_len
    inner = out_weight.shape[1]
    frames, rows = lax.axis_size("frame"), lax.axis_size("row")
    own = clip_tokens.reshape(own_count, width)
    modulation_table = jnp.transpose(modulation[0], (1, 0, 2))
    lists = tile_lists[0, 0]

    shares = RELAYED + (DIRECT,)
    starts = [own_count * sum(shares[:i]) // sum(shares) for i in range(len(shares) + 1)]
    chunks = [own[a:b] for a, b in zip(starts[:-1], starts[1:])]
    near_chunks = [lax.ppermute(c, "frame", swap_perm(frames)) for c in chunks]
    near_rows = [lax.ppermute(own, "row", swap_perm(rows))]
    if rows > 2:
        near_rows.append(lax.ppermute(near_rows[0], "row", relay_perm(rows)))

    pair_shape = (own_count, 2 * inner)
    modulate, pair_weight, out_w, own_rows, q, *pairs = pl.pallas_call(
        functools.partial(own_kernel, len(near_rows), inner),
        out_shape=[
            pltpu.VMEM((3, width), F32),
            pltpu.VMEM((width, 2 * inner), BF16),
            pltpu.VMEM((inner, width), BF16),
            pltpu.VMEM((own_count, width), BF16),
            pltpu.VMEM((own_count, inner), BF16),
        ]
        + [pltpu.VMEM(pair_shape, BF16)] * (1 + len(near_rows)),
        in_specs=[SMEM] + [HBM] * 4 + [VMEM] * len(near_rows),
        out_specs=[VMEM] * (6 + len(near_rows)),
        scratch_shapes=[
            pltpu.VMEM(modulation_table.shape, BF16),
            pltpu.VMEM((width, inner), BF16),
            pltpu.SemaphoreType.DMA((6,)),
        ],
        compiler_params=PARAMS,
        name="own_pairs",
    )(domain_ids, *map(in_hbm, (modulation_table, qkv_weight[0], out_weight[0], own)), *near_rows)

    far_chunks = []
    if frames > 2:
        *relayed, q = lax.optimization_barrier((*near_chunks[:-1], q))
        far_chunks = [lax.ppermute(c, "frame", relay_perm(frames)) for c in relayed]
        far_chunks.append(lax.ppermute(chunks[-1], "frame", far_perm(frames)))
        near_chunks = [*relayed, near_chunks[-1]]
    pairs.append(
        pl.pallas_call(
            functools.partial(pairs_kernel, len(near_chunks)),
            out_shape=pltpu.VMEM(pair_shape, BF16),
            in_specs=[VMEM] * (2 + len(near_chunks)),
            out_specs=VMEM,
            compiler_params=PARAMS,
            name="near_pairs",
        )(modulate, pair_weight, *near_chunks)
    )

    def slots_of():
        odd_frame = lax.axis_index("frame") % 2
        odd_row = lax.axis_index("row") % 2
        row_slot, frame_slot = 1, 1 + len(near_rows)
        return {
            1: frame_slot + 1 - odd_frame,
            2: frame_slot + odd_frame,
            3: row_slot + 1 - odd_row,
            4: row_slot + odd_row,
        }

    finished = pl.pallas_call(
        functools.partial(
            attend_kernel, len(pairs), len(far_chunks), inner, tile_len, slots_of
        ),
        out_shape=jax.ShapeDtypeStruct((own_count, width), BF16),
        in_specs=[SMEM] + [VMEM] * (5 + len(pairs) + len(far_chunks)),
        out_specs=VMEM,
        compiler_params=PARAMS,
        name="attend",
    )(lists, modulate, pair_weight, out_w, own_rows, q, *pairs, *far_chunks)
    segments = lax.axis_size("segment")
    return lax.ppermute(
        finished.reshape(clip_tokens.shape),
        "segment",
        [(i, (i + 1) % segments) for i in range(segments)],
    )


def solution(mesh):
    return jax.shard_map(
        body,
        mesh=mesh,
        in_specs=(
            P("segment", "frame", "row", None, None, None),
            P("segment", None, None),
            P("segment", None, None),
            P("segment", None, None, None),
            P("segment"),
            P("frame", "row", None, None),
        ),
        out_specs=P("segment", "frame", "row", None, None, None),
        check_vma=False,
    )
```

```python
import functools

import jax
import jax.numpy as jnp
from jax import lax
from jax.experimental import pallas as pl
from jax.experimental.pallas import tpu as pltpu
from jax.sharding import PartitionSpec as P

HD = 128
EPSILON = 1e-06
MASKED = -1e30
F32 = jnp.float32
BF16 = jnp.bfloat16
VMEM = pl.BlockSpec(memory_space=pltpu.VMEM)
SMEM = pl.BlockSpec(memory_space=pltpu.SMEM)
HBM = pl.BlockSpec(memory_space=pltpu.HBM)
PARAMS = pltpu.CompilerParams(vmem_limit_bytes=32 * 1024 * 1024)


def modulate_rows(domain_ref, modulation_ref):
    table = modulation_ref[...].astype(F32)
    row = lax.broadcasted_iota(jnp.int32, table.shape, 1)
    return jnp.sum(jnp.where(row == domain_ref[0], table, 0.0), axis=1)


def normalize(rows, shift, scale):
    values = rows.astype(F32)
    centered = values - jnp.mean(values, axis=-1, keepdims=True)
    row_var = jnp.mean(centered * centered, axis=-1, keepdims=True)
    return (centered * lax.rsqrt(row_var + EPSILON) * (1.0 + scale) + shift).astype(BF16)


def normalized(refs, modulate_ref):
    shift, scale = modulate_ref[0:1, :], modulate_ref[1:2, :]
    return jnp.concatenate([normalize(r[...], shift, scale) for r in refs], axis=0)


def projected(rows, weight):
    return jnp.dot(rows, weight, preferred_element_type=F32).astype(BF16)


def load_kernel(
    inner, domain_hbm, modulation_hbm, weight_hbm, out_weight_hbm, own_hbm,
    modulate_ref, q_weight_ref, pair_weight_ref, out_weight_ref, kv_ref, domain_ref, modulation_ref, own_ref, sems
):
    first = [
        pltpu.make_async_copy(modulation_hbm, modulation_ref, sems.at[0]),
        pltpu.make_async_copy(own_hbm, own_ref, sems.at[1]),
        pltpu.make_async_copy(domain_hbm, domain_ref, sems.at[6]),
    ]
    loads = [
        pltpu.make_async_copy(
            weight_hbm.at[:, pl.ds((i + 1) * inner, inner)],
            pair_weight_ref.at[:, pl.ds(i * inner, inner)],
            sems.at[2 + i],
        )
        for i in range(2)
    ]
    rest = [
        pltpu.make_async_copy(weight_hbm.at[:, pl.ds(0, inner)], q_weight_ref, sems.at[4]),
        pltpu.make_async_copy(out_weight_hbm, out_weight_ref, sems.at[5]),
    ]
    for load in first + loads + rest:
        load.start()
    for load in first:
        load.wait()
    modulate_ref[...] = modulate_rows(domain_ref, modulation_ref)
    rows = normalized((own_ref,), modulate_ref)
    for i, load in enumerate(loads):
        load.wait()
        cols = slice(i * inner, (i + 1) * inner)
        kv_ref[:, cols] = projected(rows, pair_weight_ref[:, cols])
    for load in rest:
        load.wait()


def pair_kernel(modulate_ref, weight_ref, rows_ref, kv_ref, *normed_ref):
    rows = normalized((rows_ref,), modulate_ref)
    kv_ref[...] = projected(rows, weight_ref[...])
    for ref in normed_ref:
        ref[...] = rows


def masking(lists_ref, slots, tile_len, first, key_count, query_count):
    col_tiles = query_count // tile_len
    numbers = lists_ref[...]
    slot = jnp.full(numbers.shape, slots[0], jnp.int32)
    for d in range(1, 5):
        slot = jnp.where(numbers // col_tiles == d, slots[d], slot)
    bits = jnp.sum(
        jnp.int32(1) << (slot * col_tiles + numbers % col_tiles), axis=1, keepdims=True
    )
    tile = lax.broadcasted_iota(jnp.int32, (1, query_count), 1) // tile_len
    row = jnp.zeros((1, query_count), jnp.int32)
    for t in range(col_tiles):
        row = jnp.where(tile == t, bits[t : t + 1, :], row)
    return jnp.concatenate(
        [
            jnp.broadcast_to(
                jnp.where((row >> (first + p)) & 1 == 1, 0.0, MASKED), (tile_len, query_count)
            )
            for p in range(key_count // tile_len)
        ],
        axis=0,
    )


def head_cols(h, offset=0):
    return slice(offset + h * HD, offset + (h + 1) * HD)


def scores_of(q_ref, kv_refs, bias):
    return [
        lax.dot_general(
            jnp.concatenate([r[:, head_cols(h)] for r in kv_refs], axis=0),
            q_ref[:, head_cols(h)],
            (((1,), (1,)), ((), ())),
            preferred_element_type=F32,
        )
        + bias
        for h in range(q_ref.shape[1] // HD)
    ]


def raised_from(scores, peaks):
    return [jnp.exp((s - peaks[h : h + 1]) * HD ** (-0.5)) for h, s in enumerate(scores)]


def reduced(reduce, per_head):
    return jnp.concatenate([reduce(x, axis=0, keepdims=True) for x in per_head], axis=0)


def mixes_of(kv_refs, raised):
    inner = kv_refs[0].shape[1] // 2
    return [
        lax.dot_general(
            jnp.concatenate([r[:, head_cols(h, inner)] for r in kv_refs], axis=0),
            x.astype(BF16),
            (((0,), (0,)), ((), ())),
            preferred_element_type=F32,
        )
        for h, x in enumerate(raised)
    ]


def near_kernel(n_kv, tile_len, slots_of, lists_ref, q_weight_ref, normed_ref, *refs):
    kv_refs = refs[:n_kv]
    q_ref, peak_ref, total_ref, mix_ref = refs[n_kv:]
    q_ref[...] = projected(normed_ref[...], q_weight_ref[...])
    count = normed_ref.shape[0]
    bias = masking(lists_ref, slots_of(), tile_len, 0, n_kv * count, count)
    scores = scores_of(q_ref, kv_refs, bias)
    peaks = reduced(jnp.max, scores)
    raised = raised_from(scores, peaks)
    peak_ref[...] = peaks
    total_ref[...] = reduced(jnp.sum, raised)
    for h, mix in enumerate(mixes_of(kv_refs, raised)):
        mix_ref[head_cols(h), :] = mix


def finish_kernel(
    n_kv, tile_len, slots_of, first,
    lists_ref, modulate_ref, out_weight_ref, rows_ref, q_ref, peak_ref, total_ref, mix_ref, *refs
):
    kv_refs, (finished_ref, mixed_ref) = refs[:n_kv], refs[n_kv:]
    count = rows_ref.shape[0]
    bias = masking(lists_ref, slots_of(), tile_len, first, n_kv * count, count)
    scores = scores_of(q_ref, kv_refs, bias)
    before = peak_ref[...]
    peaks = jnp.maximum(reduced(jnp.max, scores), before)
    raised = raised_from(scores, peaks)
    kept = jnp.exp((before - peaks) * HD ** (-0.5))
    share = 1.0 / (total_ref[...] * kept + reduced(jnp.sum, raised))
    kept = kept * share
    for h, mix in enumerate(mixes_of(kv_refs, raised)):
        mixed_ref[head_cols(h), :] = (
            mix_ref[head_cols(h), :] * kept[h : h + 1] + mix * share[h : h + 1]
        ).astype(BF16)
    branch = lax.dot_general(
        mixed_ref[...],
        out_weight_ref[...],
        (((0,), (0,)), ((), ())),
        preferred_element_type=F32,
    )
    finished_ref[...] = (rows_ref[...].astype(F32) + modulate_ref[2:3, :] * branch).astype(BF16)


def swap_perm(size):
    return [(i, i ^ 1) for i in range(size)]


def relay_perm(size):
    return [(i, i + 2) for i in range(0, size - 2, 2)] + [(i, i - 2) for i in range(3, size, 2)]


def beyond_perm(size):
    return [((i + (2 if i % 2 == 0 else -2)) % size, i) for i in range(size)]


def in_hbm(x):
    return pltpu.with_memory_space_constraint(x, pltpu.HBM)


def after(x, *others):
    return lax.optimization_barrier((x, *others))[0]


def call(kernel, ins, outs, args, scratch=(), name=None):
    return pl.pallas_call(
        kernel,
        out_shape=outs,
        in_specs=ins,
        out_specs=[VMEM] * len(outs),
        scratch_shapes=scratch,
        compiler_params=PARAMS,
        name=name,
    )(*args)


def body(clip_tokens, qkv_weight, out_weight, modulation, domain_ids, tile_lists):
    col_tiles, tile_len, width = clip_tokens.shape[3:]
    own_count = col_tiles * tile_len
    inner = out_weight.shape[1]
    heads = inner // HD
    frames, rows = lax.axis_size("frame"), lax.axis_size("row")
    segments = lax.axis_size("segment")
    modulation_table = jnp.transpose(modulation[0], (1, 0, 2))
    weight = qkv_weight[0]
    own = clip_tokens.reshape(own_count, width)

    def held(count, wide, dtype=BF16):
        return pltpu.VMEM((count, wide), dtype)

    tokens = lax.ppermute(own, "frame", swap_perm(frames))
    beyond = [lax.ppermute(own, "frame", beyond_perm(frames))] if frames > 2 else []
    lists = lax.ppermute(tile_lists[0, 0], "frame", swap_perm(frames))

    modulate, q_weight, pair_weight, out_w, kv_own = call(
        functools.partial(load_kernel, inner),
        [pl.BlockSpec(memory_space=pl.ANY)] + [HBM] * 4,
        [
            held(3, width, F32),
            held(width, inner),
            held(width, 2 * inner),
            held(inner, width),
            held(own_count, 2 * inner),
        ],
        [domain_ids, *map(in_hbm, (modulation_table, weight, out_weight[0], own))],
        [
            pltpu.SMEM(domain_ids.shape, jnp.int32),
            pltpu.VMEM(modulation_table.shape, BF16),
            pltpu.VMEM((own_count, width), BF16),
            pltpu.SemaphoreType.DMA((7,)),
        ],
        "own_pairs",
    )

    def slots_of():
        odd_frame = 1 - lax.axis_index("frame") % 2
        odd_row = lax.axis_index("row") % 2
        row_slot = 2 + len(beyond)
        return [
            0,
            2 - odd_frame,
            1 + odd_frame,
            row_slot + 1 - odd_row,
            row_slot + odd_row,
        ]

    def pairs_of(arrived, name, with_rows=False):
        outs = [held(own_count, 2 * inner)] + [held(own_count, width)] * with_rows
        return call(pair_kernel, [VMEM] * 3, outs, [modulate, pair_weight, arrived], name=name)

    tokens, lists = lax.optimization_barrier((tokens, lists, kv_own))[:2]
    kv_tokens, normed = pairs_of(tokens, "pairs", True)
    kv_rows = [lax.ppermute(kv_tokens, "row", swap_perm(rows))]
    if rows > 2:
        kv_rows.append(lax.ppermute(kv_rows[0], "row", relay_perm(rows)))
    kv_beyond = [pairs_of(after(b, kv_tokens), "beyond_pairs")[0] for b in beyond]
    near = [kv_tokens, kv_own, *kv_beyond]
    q, *partial = call(
        functools.partial(near_kernel, len(near), tile_len, slots_of),
        [VMEM] * (3 + len(near)),
        [
            held(own_count, inner),
            held(heads, own_count, F32),
            held(heads, own_count, F32),
            held(inner, own_count, F32),
        ],
        [lists, q_weight, normed, *near],
        name="near_attention",
    )
    (finished,) = call(
        functools.partial(
            finish_kernel, len(kv_rows), tile_len, slots_of, len(near) * col_tiles
        ),
        [VMEM] * (8 + len(kv_rows)),
        [jax.ShapeDtypeStruct((own_count, width), BF16)],
        [lists, modulate, out_w, tokens, q, *partial, *kv_rows],
        [pltpu.VMEM((inner, own_count), BF16)],
        name="finish",
    )
    onward = [
        (s * frames + f, (s + 1) % segments * frames + (f ^ 1))
        for s in range(segments)
        for f in range(frames)
    ]
    return lax.ppermute(finished.reshape(clip_tokens.shape), ("segment", "frame"), onward)


def solution(mesh):
    return jax.shard_map(
        body,
        mesh=mesh,
        in_specs=(
            P("segment", "frame", "row", None, None, None),
            P("segment", None, None),
            P("segment", None, None),
            P("segment", None, None, None),
            P("segment"),
            P("frame", "row", None, None),
        ),
        out_specs=P("segment", "frame", "row", None, None, None),
        check_vma=False,
    )
```

```python
import functools

import jax
import jax.numpy as jnp
from jax import lax
from jax.experimental import pallas as pl
from jax.experimental.pallas import tpu as pltpu
from jax.sharding import PartitionSpec as P

HD = 128
EPSILON = 1e-06
MASKED = -1e30
RAW = 4
LOADS = 4
F32 = jnp.float32
BF16 = jnp.bfloat16
VMEM = pl.BlockSpec(memory_space=pltpu.VMEM)
SMEM = pl.BlockSpec(memory_space=pltpu.SMEM)
HBM = pl.BlockSpec(memory_space=pltpu.HBM)
PARAMS = pltpu.CompilerParams(vmem_limit_bytes=32 * 1024 * 1024)


def modulate_rows(domain_ref, modulation_ref):
    table = modulation_ref[...].astype(F32)
    row = lax.broadcasted_iota(jnp.int32, table.shape, 1)
    return jnp.sum(jnp.where(row == domain_ref[0], table, 0.0), axis=1)


def normalize(rows, shift, scale):
    values = rows.astype(F32)
    centered = values - jnp.mean(values, axis=-1, keepdims=True)
    row_var = jnp.mean(centered * centered, axis=-1, keepdims=True)
    return (centered * lax.rsqrt(row_var + EPSILON) * (1.0 + scale) + shift).astype(BF16)


def normalized(refs, modulate_ref):
    shift, scale = modulate_ref[0:1, :], modulate_ref[1:2, :]
    return jnp.concatenate([normalize(r[...], shift, scale) for r in refs], axis=0)


def projected(rows, weight):
    return jnp.dot(rows, weight, preferred_element_type=F32).astype(BF16)


def load_kernel(
    inner, domain_hbm, modulation_hbm, weight_hbm, own_hbm,
    modulate_ref, weight_ref, kv_ref, *refs
):
    *tail_ref, domain_ref, modulation_ref, own_ref, sems = refs
    first = [
        pltpu.make_async_copy(domain_hbm, domain_ref, sems.at[0]),
        pltpu.make_async_copy(modulation_hbm, modulation_ref, sems.at[1]),
        pltpu.make_async_copy(own_hbm, own_ref, sems.at[2]),
    ]
    part = 2 * inner // LOADS
    loads = [
        pltpu.make_async_copy(
            weight_hbm.at[:, pl.ds(inner + i * part, part)],
            weight_ref.at[:, pl.ds(i * part, part)],
            sems.at[3 + i],
        )
        for i in range(LOADS)
    ]
    for load in first + loads:
        load.start()
    for load in first:
        load.wait()
    modulate_ref[...] = modulate_rows(domain_ref, modulation_ref)
    rows = normalized((own_ref,), modulate_ref)
    for i, load in enumerate(loads):
        load.wait()
        cols = slice(i * part, (i + 1) * part)
        pairs = projected(rows, weight_ref[:, cols])
        kv_ref[:, cols] = pairs
        for ref in tail_ref:
            ref[:, cols] = pairs[rows.shape[0] - ref.shape[0] :]


def beyond_kernel(inner, n_rows, weight_hbm, out_weight_hbm, modulate_ref, pair_weight_ref, *refs):
    rows_refs, (q_weight_ref, out_weight_ref) = refs[:n_rows], refs[n_rows : n_rows + 2]
    *kv_refs, sems = refs[n_rows + 2 :]
    loads = [
        pltpu.make_async_copy(weight_hbm.at[:, pl.ds(0, inner)], q_weight_ref, sems.at[0]),
        pltpu.make_async_copy(out_weight_hbm, out_weight_ref, sems.at[1]),
    ]
    for load in loads:
        load.start()
    for rows_ref, kv_ref in zip(rows_refs, kv_refs):
        kv_ref[...] = projected(normalized((rows_ref,), modulate_ref), pair_weight_ref[...])
    for load in loads:
        load.wait()


def pair_kernel(modulate_ref, weight_ref, rows_ref, kv_ref, normed_ref):
    rows = normalized((rows_ref,), modulate_ref)
    normed_ref[...] = rows
    kv_ref[...] = projected(rows, weight_ref[...])


def masking(lists_ref, slots, tile_len, first, key_count, query_count):
    col_tiles = query_count // tile_len
    numbers = lists_ref[...]
    slot = jnp.full(numbers.shape, slots[0], jnp.int32)
    for d in range(1, 5):
        slot = jnp.where(numbers // col_tiles == d, slots[d], slot)
    bits = jnp.sum(
        jnp.int32(1) << (slot * col_tiles + numbers % col_tiles), axis=1, keepdims=True
    )
    tile = lax.broadcasted_iota(jnp.int32, (1, query_count), 1) // tile_len
    row = jnp.zeros((1, query_count), jnp.int32)
    for t in range(col_tiles):
        row = jnp.where(tile == t, bits[t : t + 1, :], row)
    return jnp.concatenate(
        [
            jnp.broadcast_to(
                jnp.where((row >> (first + p)) & 1 == 1, 0.0, MASKED), (tile_len, query_count)
            )
            for p in range(key_count // tile_len)
        ],
        axis=0,
    )


def head_cols(h, offset=0):
    return slice(offset + h * HD, offset + (h + 1) * HD)


def scores_of(q_ref, kv_refs, bias):
    return [
        lax.dot_general(
            jnp.concatenate([r[:, head_cols(h)] for r in kv_refs], axis=0),
            q_ref[:, head_cols(h)],
            (((1,), (1,)), ((), ())),
            preferred_element_type=F32,
        )
        + bias
        for h in range(q_ref.shape[1] // HD)
    ]


def raised_from(scores, peaks):
    return [jnp.exp((s - peaks[h : h + 1]) * HD ** (-0.5)) for h, s in enumerate(scores)]


def reduced(reduce, per_head):
    return jnp.concatenate([reduce(x, axis=0, keepdims=True) for x in per_head], axis=0)


def mixes_of(kv_refs, raised):
    inner = kv_refs[0].shape[1] // 2
    return [
        lax.dot_general(
            jnp.concatenate([r[:, head_cols(h, inner)] for r in kv_refs], axis=0),
            x.astype(BF16),
            (((0,), (0,)), ((), ())),
            preferred_element_type=F32,
        )
        for h, x in enumerate(raised)
    ]


def near_kernel(n_kv, tile_len, slots_of, lists_ref, q_weight_ref, normed_ref, *refs):
    kv_refs = refs[:n_kv]
    q_ref, peak_ref, total_ref, mix_ref = refs[n_kv:]
    q_ref[...] = projected(normed_ref[...], q_weight_ref[...])
    count, key_count = normed_ref.shape[0], sum(r.shape[0] for r in kv_refs)
    bias = masking(lists_ref, slots_of(), tile_len, 0, key_count, count)
    scores = scores_of(q_ref, kv_refs, bias)
    peaks = reduced(jnp.max, scores)
    raised = raised_from(scores, peaks)
    peak_ref[...] = peaks
    total_ref[...] = reduced(jnp.sum, raised)
    for h, mix in enumerate(mixes_of(kv_refs, raised)):
        mix_ref[head_cols(h), :] = mix


def finish_kernel(
    n_kv, tile_len, slots_of, first,
    lists_ref, modulate_ref, out_weight_ref, rows_ref, q_ref, peak_ref, total_ref, mix_ref, *refs
):
    kv_refs, (finished_ref, mixed_ref) = refs[:n_kv], refs[n_kv:]
    count = rows_ref.shape[0]
    bias = masking(lists_ref, slots_of(), tile_len, first, n_kv * count, count)
    scores = scores_of(q_ref, kv_refs, bias)
    before = peak_ref[...]
    peaks = jnp.maximum(reduced(jnp.max, scores), before)
    raised = raised_from(scores, peaks)
    kept = jnp.exp((before - peaks) * HD ** (-0.5))
    share = 1.0 / (total_ref[...] * kept + reduced(jnp.sum, raised))
    kept = kept * share
    for h, mix in enumerate(mixes_of(kv_refs, raised)):
        mixed_ref[head_cols(h), :] = (
            mix_ref[head_cols(h), :] * kept[h : h + 1] + mix * share[h : h + 1]
        ).astype(BF16)
    branch = lax.dot_general(
        mixed_ref[...],
        out_weight_ref[...],
        (((0,), (0,)), ((), ())),
        preferred_element_type=F32,
    )
    finished_ref[...] = (rows_ref[...].astype(F32) + modulate_ref[2:3, :] * branch).astype(BF16)


def swap_perm(size):
    return [(i, i ^ 1) for i in range(size)]


def relay_perm(size):
    return [(i, i + 2) for i in range(0, size - 2, 2)] + [(i, i - 2) for i in range(3, size, 2)]


def beyond_perm(size):
    return [((i + (2 if i % 2 == 0 else -2)) % size, i) for i in range(size)]


def in_hbm(x):
    return pltpu.with_memory_space_constraint(x, pltpu.HBM)


def after(x, *others):
    return lax.optimization_barrier((x, *others))[0]


def call(kernel, ins, outs, args, scratch=(), name=None, weight=1):
    return pl.pallas_call(
        kernel,
        out_shape=outs,
        in_specs=ins,
        out_specs=[VMEM] * len(outs),
        scratch_shapes=scratch,
        compiler_params=PARAMS,
        cost_estimate=pl.CostEstimate(flops=weight, bytes_accessed=0, transcendentals=0),
        name=name,
    )(*args)


def body(clip_tokens, qkv_weight, out_weight, modulation, domain_ids, tile_lists):
    col_tiles, tile_len, width = clip_tokens.shape[3:]
    own_count = col_tiles * tile_len
    inner = out_weight.shape[1]
    heads = inner // HD
    frames, rows = lax.axis_size("frame"), lax.axis_size("row")
    segments = lax.axis_size("segment")
    modulation_table = jnp.transpose(modulation[0], (1, 0, 2))
    weight = qkv_weight[0]
    own = clip_tokens.reshape(own_count, width)

    def held(count, wide, dtype=BF16):
        return pltpu.VMEM((count, wide), dtype)

    def from_partner(x):
        return lax.ppermute(x, "frame", swap_perm(frames))

    def from_beyond(x):
        return lax.ppermute(x, "frame", beyond_perm(frames))

    tokens = from_partner(own)
    lists = from_partner(tile_lists[0, 0])
    far = frames > 2
    sent = own_count * RAW // 8
    beyond = [from_beyond(own[:sent])] if far else []

    modulate, pair_weight, kv_own, *tail = call(
        functools.partial(load_kernel, inner),
        [pl.BlockSpec(memory_space=pl.ANY)] + [HBM] * 3,
        [held(3, width, F32), held(width, 2 * inner), held(own_count, 2 * inner)]
        + [held(own_count - sent, 2 * inner)] * far,
        [domain_ids, *map(in_hbm, (modulation_table, weight, own))],
        [
            pltpu.SMEM(domain_ids.shape, jnp.int32),
            pltpu.VMEM(modulation_table.shape, BF16),
            pltpu.VMEM((own_count, width), BF16),
            pltpu.SemaphoreType.DMA((3 + LOADS,)),
        ],
        "own_pairs",
    )
    kv_tail = [from_beyond(t) for t in tail]
    q_weight, out_w, *kv_beyond = call(
        functools.partial(beyond_kernel, inner, len(beyond)),
        [HBM] * 2 + [VMEM] * (2 + len(beyond)),
        [held(width, inner), held(inner, width)] + [held(sent, 2 * inner)] * far,
        [in_hbm(weight), in_hbm(out_weight[0]), modulate, pair_weight, *beyond],
        [pltpu.SemaphoreType.DMA((2,))],
        "beyond_pairs",
    )
    kv_beyond += kv_tail
    near_tiles = 2 + far

    def slots_of():
        odd_frame = 1 - lax.axis_index("frame") % 2
        odd_row = lax.axis_index("row") % 2
        return [
            0,
            2 - odd_frame,
            1 + odd_frame,
            near_tiles + 1 - odd_row,
            near_tiles + odd_row,
        ]

    tokens = after(tokens, q_weight)
    kv_tokens, normed = call(
        pair_kernel,
        [VMEM] * 3,
        [held(own_count, 2 * inner), held(own_count, width)],
        [modulate, pair_weight, tokens],
        name="pairs",
    )
    kv_rows = [lax.ppermute(kv_tokens, "row", swap_perm(rows))]
    if rows > 2:
        kv_rows.append(lax.ppermute(kv_rows[0], "row", relay_perm(rows)))
    near = [kv_tokens, kv_own, *kv_beyond]
    q, *partial = call(
        functools.partial(near_kernel, len(near), tile_len, slots_of),
        [VMEM] * (3 + len(near)),
        [
            held(own_count, inner),
            held(heads, own_count, F32),
            held(heads, own_count, F32),
            held(inner, own_count, F32),
        ],
        [lists, q_weight, normed, *near],
        name="near_attention",
        weight=10**10,
    )
    (finished,) = call(
        functools.partial(
            finish_kernel, len(kv_rows), tile_len, slots_of, near_tiles * col_tiles
        ),
        [VMEM] * (8 + len(kv_rows)),
        [jax.ShapeDtypeStruct((own_count, width), BF16)],
        [lists, modulate, out_w, tokens, q, *partial, *kv_rows],
        [pltpu.VMEM((inner, own_count), BF16)],
        "finish",
    )
    onward = [
        (s * frames + f, (s + 1) % segments * frames + (f ^ 1))
        for s in range(segments)
        for f in range(frames)
    ]
    return lax.ppermute(finished.reshape(clip_tokens.shape), ("segment", "frame"), onward)


def solution(mesh):
    return jax.shard_map(
        body,
        mesh=mesh,
        in_specs=(
            P("segment", "frame", "row", None, None, None),
            P("segment", None, None),
            P("segment", None, None),
            P("segment", None, None, None),
            P("segment"),
            P("frame", "row", None, None),
        ),
        out_specs=P("segment", "frame", "row", None, None, None),
        check_vma=False,
    )
```

```python
import functools

import jax
import jax.numpy as jnp
from jax import lax
from jax.experimental import pallas as pl
from jax.experimental.pallas import tpu as pltpu
from jax.sharding import PartitionSpec as P

HD = 128
EPSILON = 1e-06
MASKED = -1e30
RAW = 4
LOADS = 4
FIRST = 7
F32 = jnp.float32
BF16 = jnp.bfloat16
VMEM = pl.BlockSpec(memory_space=pltpu.VMEM)
SMEM = pl.BlockSpec(memory_space=pltpu.SMEM)
HBM = pl.BlockSpec(memory_space=pltpu.HBM)
PARAMS = pltpu.CompilerParams(vmem_limit_bytes=32 * 1024 * 1024)


def modulate_rows(domain_ref, modulation_ref):
    table = modulation_ref[...].astype(F32)
    row = lax.broadcasted_iota(jnp.int32, table.shape, 1)
    return jnp.sum(jnp.where(row == domain_ref[0], table, 0.0), axis=1)


def normalize(rows, shift, scale):
    values = rows.astype(F32)
    centered = values - jnp.mean(values, axis=-1, keepdims=True)
    row_var = jnp.mean(centered * centered, axis=-1, keepdims=True)
    return (centered * lax.rsqrt(row_var + EPSILON) * (1.0 + scale) + shift).astype(BF16)


def normalized(refs, modulate_ref):
    shift, scale = modulate_ref[0:1, :], modulate_ref[1:2, :]
    return jnp.concatenate([normalize(r[...], shift, scale) for r in refs], axis=0)


def projected(rows, weight):
    return jnp.dot(rows, weight, preferred_element_type=F32).astype(BF16)


def load_kernel(
    inner, domain_hbm, modulation_hbm, weight_hbm, own_hbm,
    modulate_ref, q_weight_ref, weight_ref, kv_ref, *refs
):
    *tail_ref, domain_ref, modulation_ref, own_ref, sems = refs
    first = [
        pltpu.make_async_copy(domain_hbm, domain_ref, sems.at[0]),
        pltpu.make_async_copy(modulation_hbm, modulation_ref, sems.at[1]),
        pltpu.make_async_copy(own_hbm, own_ref, sems.at[2]),
    ]
    part = 2 * inner // LOADS
    loads = [
        pltpu.make_async_copy(
            weight_hbm.at[:, pl.ds(inner + i * part, part)],
            weight_ref.at[:, pl.ds(i * part, part)],
            sems.at[3 + i],
        )
        for i in range(LOADS)
    ]
    query = pltpu.make_async_copy(weight_hbm.at[:, pl.ds(0, inner)], q_weight_ref, sems.at[3 + LOADS])
    for load in first + loads + [query]:
        load.start()
    for load in first:
        load.wait()
    modulate_ref[...] = modulate_rows(domain_ref, modulation_ref)
    rows = normalized((own_ref,), modulate_ref)
    for i, load in enumerate(loads):
        load.wait()
        cols = slice(i * part, (i + 1) * part)
        pairs = projected(rows, weight_ref[:, cols])
        kv_ref[:, cols] = pairs
        for ref in tail_ref:
            ref[:, cols] = pairs[rows.shape[0] - ref.shape[0] :]
    query.wait()


def beyond_kernel(modulate_ref, weight_ref, rows_ref, kv_ref):
    kv_ref[...] = projected(normalized((rows_ref,), modulate_ref), weight_ref[...])


def pair_kernel(modulate_ref, weight_ref, rows_ref, kv_ref, normed_ref):
    rows = normalized((rows_ref,), modulate_ref)
    normed_ref[...] = rows
    kv_ref[...] = projected(rows, weight_ref[...])


def masking(lists_ref, slots, tile_len, first, key_count, query_count):
    col_tiles = query_count // tile_len
    numbers = lists_ref[...]
    slot = jnp.full(numbers.shape, slots[0], jnp.int32)
    for d in range(1, 5):
        slot = jnp.where(numbers // col_tiles == d, slots[d], slot)
    bits = jnp.sum(
        jnp.int32(1) << (slot * col_tiles + numbers % col_tiles), axis=1, keepdims=True
    )
    tile = lax.broadcasted_iota(jnp.int32, (1, query_count), 1) // tile_len
    row = jnp.zeros((1, query_count), jnp.int32)
    for t in range(col_tiles):
        row = jnp.where(tile == t, bits[t : t + 1, :], row)
    parts, end = [], first + key_count
    for p in range(first // tile_len, pl.cdiv(end, tile_len)):
        size = min(end, (p + 1) * tile_len) - max(first, p * tile_len)
        added = jnp.where((row >> p) & 1 == 1, 0.0, MASKED)
        parts.append(jnp.broadcast_to(added, (size, query_count)))
    return jnp.concatenate(parts, axis=0)


def head_cols(h, offset=0):
    return slice(offset + h * HD, offset + (h + 1) * HD)


def scores_of(q_ref, kv_refs, bias):
    return [
        lax.dot_general(
            jnp.concatenate([r[:, head_cols(h)] for r in kv_refs], axis=0),
            q_ref[:, head_cols(h)],
            (((1,), (1,)), ((), ())),
            preferred_element_type=F32,
        )
        + bias
        for h in range(q_ref.shape[1] // HD)
    ]


def raised_from(scores, peaks):
    return [jnp.exp((s - peaks[h : h + 1]) * HD ** (-0.5)) for h, s in enumerate(scores)]


def reduced(reduce, per_head):
    return jnp.concatenate([reduce(x, axis=0, keepdims=True) for x in per_head], axis=0)


def mixes_of(kv_refs, raised):
    inner = kv_refs[0].shape[1] // 2
    return [
        lax.dot_general(
            jnp.concatenate([r[:, head_cols(h, inner)] for r in kv_refs], axis=0),
            x.astype(BF16),
            (((0,), (0,)), ((), ())),
            preferred_element_type=F32,
        )
        for h, x in enumerate(raised)
    ]


def near_kernel(n_kv, tile_len, slots_of, lists_ref, q_weight_ref, _, normed_ref, *refs):
    kv_refs = refs[:n_kv]
    q_ref, peak_ref, total_ref, mix_ref = refs[n_kv:]
    q_ref[...] = projected(normed_ref[...], q_weight_ref[...])
    count, key_count = normed_ref.shape[0], sum(r.shape[0] for r in kv_refs)
    bias = masking(lists_ref, slots_of(), tile_len, 0, key_count, count)
    scores = scores_of(q_ref, kv_refs, bias)
    peaks = reduced(jnp.max, scores)
    raised = raised_from(scores, peaks)
    peak_ref[...] = peaks
    total_ref[...] = reduced(jnp.sum, raised)
    for h, mix in enumerate(mixes_of(kv_refs, raised)):
        mix_ref[head_cols(h), :] = mix


def finish_kernel(
    n_kv, tile_len, slots_of, first,
    lists_ref, modulate_ref, out_weight_ref, rows_ref, q_ref, peak_ref, total_ref, mix_ref, *refs
):
    kv_refs, (mixed_ref, finished_ref) = refs[:n_kv], refs[n_kv:]
    count = rows_ref.shape[0]
    key_count = sum(r.shape[0] for r in kv_refs)
    bias = masking(lists_ref, slots_of(), tile_len, first, key_count, count)
    scores = scores_of(q_ref, kv_refs, bias)
    before = peak_ref[...]
    peaks = jnp.maximum(reduced(jnp.max, scores), before)
    raised = raised_from(scores, peaks)
    kept = jnp.exp((before - peaks) * HD ** (-0.5))
    share = 1.0 / (total_ref[...] * kept + reduced(jnp.sum, raised))
    kept = kept * share
    for h, mix in enumerate(mixes_of(kv_refs, raised)):
        mixed_ref[head_cols(h), :] = (
            mix_ref[head_cols(h), :] * kept[h : h + 1] + mix * share[h : h + 1]
        ).astype(BF16)
    output_columns(0, mixed_ref, modulate_ref, out_weight_ref, rows_ref, finished_ref)


def output_columns(first, mixed_ref, modulate_ref, out_weight_ref, rows_ref, finished_ref):
    cols = slice(first, first + finished_ref.shape[1])
    branch = lax.dot_general(
        mixed_ref[...],
        out_weight_ref[:, cols],
        (((0,), (0,)), ((), ())),
        preferred_element_type=F32,
    )
    finished_ref[...] = (
        rows_ref[:, cols].astype(F32) + modulate_ref[2:3, cols] * branch
    ).astype(BF16)


def swap_perm(size):
    return [(i, i ^ 1) for i in range(size)]


def relay_perm(size):
    return [(i, i + 2) for i in range(0, size - 2, 2)] + [(i, i - 2) for i in range(3, size, 2)]


def beyond_perm(size):
    return [((i + (2 if i % 2 == 0 else -2)) % size, i) for i in range(size)]


def in_hbm(x):
    return pltpu.with_memory_space_constraint(x, pltpu.HBM)


def after(x, *others):
    return lax.optimization_barrier((x, *others))[0]


def call(kernel, ins, outs, args, scratch=(), name=None, weight=1):
    return pl.pallas_call(
        kernel,
        out_shape=outs,
        in_specs=ins,
        out_specs=[VMEM] * len(outs),
        scratch_shapes=scratch,
        compiler_params=PARAMS,
        cost_estimate=pl.CostEstimate(flops=weight, bytes_accessed=0, transcendentals=0),
        name=name,
    )(*args)


def body(clip_tokens, qkv_weight, out_weight, modulation, domain_ids, tile_lists):
    col_tiles, tile_len, width = clip_tokens.shape[3:]
    own_count = col_tiles * tile_len
    inner = out_weight.shape[1]
    heads = inner // HD
    frames, rows = lax.axis_size("frame"), lax.axis_size("row")
    segments = lax.axis_size("segment")
    modulation_table = jnp.transpose(modulation[0], (1, 0, 2))
    weight = qkv_weight[0]
    own = clip_tokens.reshape(own_count, width)

    def held(count, wide, dtype=BF16):
        return pltpu.VMEM((count, wide), dtype)

    def from_partner(x):
        return lax.ppermute(x, "frame", swap_perm(frames))

    def from_beyond(x):
        return lax.ppermute(x, "frame", beyond_perm(frames))

    tokens = from_partner(own)
    lists = from_partner(tile_lists[0, 0])
    far = frames > 2
    sent = own_count * RAW // 8
    beyond = [from_beyond(own[:sent])] if far else []

    modulate, q_weight, pair_weight, kv_own, *tail = call(
        functools.partial(load_kernel, inner),
        [pl.BlockSpec(memory_space=pl.ANY)] + [HBM] * 3,
        [held(3, width, F32), held(width, inner), held(width, 2 * inner), held(own_count, 2 * inner)]
        + [held(own_count - sent, 2 * inner)] * far,
        [domain_ids, *map(in_hbm, (modulation_table, weight, own))],
        [
            pltpu.SMEM(domain_ids.shape, jnp.int32),
            pltpu.VMEM(modulation_table.shape, BF16),
            pltpu.VMEM((own_count, width), BF16),
            pltpu.SemaphoreType.DMA((4 + LOADS,)),
        ],
        "own_pairs",
    )
    kv_tail = [from_beyond(t) for t in tail]
    kv_beyond = [
        call(
            beyond_kernel,
            [VMEM] * 3,
            [held(sent, 2 * inner)],
            [modulate, pair_weight, b],
            name="beyond_pairs",
        )[0]
        for b in beyond
    ]
    near_tiles = 2 + far

    def slots_of():
        odd_frame = 1 - lax.axis_index("frame") % 2
        odd_row = lax.axis_index("row") % 2
        return [
            0,
            2 - odd_frame,
            1 + odd_frame,
            near_tiles + 1 - odd_row,
            near_tiles + odd_row,
        ]

    tokens = after(tokens, kv_own, *kv_beyond)
    kv_tokens, normed = call(
        pair_kernel,
        [VMEM] * 3,
        [held(own_count, 2 * inner), held(own_count, width)],
        [modulate, pair_weight, tokens],
        name="pairs",
    )
    kv_rows = [lax.ppermute(kv_tokens, "row", swap_perm(rows))]
    if rows > 2:
        kv_rows.append(lax.ppermute(kv_rows[0], "row", relay_perm(rows)))
    near = [kv_tokens, kv_own, *kv_beyond]
    q, *partial = call(
        functools.partial(near_kernel, len(near), tile_len, slots_of),
        [VMEM] * (4 + len(near)),
        [
            held(own_count, inner),
            held(heads, own_count, F32),
            held(heads, own_count, F32),
            held(inner, own_count, F32),
        ],
        [lists, q_weight, out_weight[0], normed, *near],
        name="near_attention",
        weight=10**10,
    )
    late = [*kv_tail, *kv_rows]
    first_cols = width * FIRST // 12
    mixed, *finished = call(
        functools.partial(
            finish_kernel, len(late), tile_len, slots_of, sum(x.shape[0] for x in near)
        ),
        [VMEM] * (8 + len(late)),
        [held(inner, own_count), held(own_count, first_cols)],
        [lists, modulate, out_weight[0], tokens, q, *partial, *late],
        name="finish",
    )
    finished += call(
        functools.partial(output_columns, first_cols),
        [VMEM] * 4,
        [held(own_count, width - first_cols)],
        [mixed, modulate, out_weight[0], tokens],
        name="finish_rest",
    )
    onward = [
        (s * frames + f, (s + 1) % segments * frames + (f ^ 1))
        for s in range(segments)
        for f in range(frames)
    ]
    handed = [lax.ppermute(x, ("segment", "frame"), onward) for x in finished]
    return jnp.concatenate(handed, axis=1).reshape(clip_tokens.shape)


def solution(mesh):
    return jax.shard_map(
        body,
        mesh=mesh,
        in_specs=(
            P("segment", "frame", "row", None, None, None),
            P("segment", None, None),
            P("segment", None, None),
            P("segment", None, None, None),
            P("segment"),
            P("frame", "row", None, None),
        ),
        out_specs=P("segment", "frame", "row", None, None, None),
        check_vma=False,
    )
```

```python
import functools

import jax
import jax.numpy as jnp
from jax import lax
from jax.experimental import pallas as pl
from jax.experimental.pallas import tpu as pltpu
from jax.sharding import PartitionSpec as P

HD = 128
EPSILON = 1e-06
MASKED = -1e30
RAW = 5
LOADS = 4
FIRST = 7
F32 = jnp.float32
BF16 = jnp.bfloat16
VMEM = pl.BlockSpec(memory_space=pltpu.VMEM)
SMEM = pl.BlockSpec(memory_space=pltpu.SMEM)
HBM = pl.BlockSpec(memory_space=pltpu.HBM)
PARAMS = pltpu.CompilerParams(vmem_limit_bytes=32 * 1024 * 1024)


def modulate_rows(domain_ref, modulation_ref):
    table = modulation_ref[...].astype(F32)
    row = lax.broadcasted_iota(jnp.int32, table.shape, 1)
    return jnp.sum(jnp.where(row == domain_ref[0], table, 0.0), axis=1)


def normalize(rows, shift, scale):
    values = rows.astype(F32)
    centered = values - jnp.mean(values, axis=-1, keepdims=True)
    row_var = jnp.mean(centered * centered, axis=-1, keepdims=True)
    return (centered * lax.rsqrt(row_var + EPSILON) * (1.0 + scale) + shift).astype(BF16)


def normalized(refs, modulate_ref):
    shift, scale = modulate_ref[0:1, :], modulate_ref[1:2, :]
    return jnp.concatenate([normalize(r[...], shift, scale) for r in refs], axis=0)


def projected(rows, weight):
    return jnp.dot(rows, weight, preferred_element_type=F32).astype(BF16)


def load_kernel(
    inner, domain_hbm, modulation_hbm, weight_hbm, own_hbm,
    modulate_ref, q_weight_ref, weight_ref, kv_ref, *refs
):
    *tail_ref, domain_ref, modulation_ref, own_ref, sems = refs
    first = [
        pltpu.make_async_copy(domain_hbm, domain_ref, sems.at[0]),
        pltpu.make_async_copy(modulation_hbm, modulation_ref, sems.at[1]),
        pltpu.make_async_copy(own_hbm, own_ref, sems.at[2]),
    ]
    part = 2 * inner // LOADS
    loads = [
        pltpu.make_async_copy(
            weight_hbm.at[:, pl.ds(inner + i * part, part)],
            weight_ref.at[:, pl.ds(i * part, part)],
            sems.at[3 + i],
        )
        for i in range(LOADS)
    ]
    query = pltpu.make_async_copy(weight_hbm.at[:, pl.ds(0, inner)], q_weight_ref, sems.at[3 + LOADS])
    for load in first + loads + [query]:
        load.start()
    for load in first:
        load.wait()
    modulate_ref[...] = modulate_rows(domain_ref, modulation_ref)
    rows = normalized((own_ref,), modulate_ref)
    for i, load in enumerate(loads):
        load.wait()
        cols = slice(i * part, (i + 1) * part)
        pairs = projected(rows, weight_ref[:, cols])
        kv_ref[:, cols] = pairs
        for ref in tail_ref:
            ref[:, cols] = pairs[rows.shape[0] - ref.shape[0] :]
    query.wait()


def beyond_kernel(modulate_ref, weight_ref, rows_ref, kv_ref):
    kv_ref[...] = projected(normalized((rows_ref,), modulate_ref), weight_ref[...])


def pair_kernel(modulate_ref, weight_ref, rows_ref, kv_ref, normed_ref):
    rows = normalized((rows_ref,), modulate_ref)
    normed_ref[...] = rows
    kv_ref[...] = projected(rows, weight_ref[...])


def masking(lists_ref, slots, tile_len, first, key_count, query_count):
    col_tiles = query_count // tile_len
    numbers = lists_ref[...]
    slot = jnp.full(numbers.shape, slots[0], jnp.int32)
    for d in range(1, 5):
        slot = jnp.where(numbers // col_tiles == d, slots[d], slot)
    bits = jnp.sum(
        jnp.int32(1) << (slot * col_tiles + numbers % col_tiles), axis=1, keepdims=True
    )
    tile = lax.broadcasted_iota(jnp.int32, (1, query_count), 1) // tile_len
    row = jnp.zeros((1, query_count), jnp.int32)
    for t in range(col_tiles):
        row = jnp.where(tile == t, bits[t : t + 1, :], row)
    parts, end = [], first + key_count
    for p in range(first // tile_len, pl.cdiv(end, tile_len)):
        size = min(end, (p + 1) * tile_len) - max(first, p * tile_len)
        added = jnp.where((row >> p) & 1 == 1, 0.0, MASKED)
        parts.append(jnp.broadcast_to(added, (size, query_count)))
    return jnp.concatenate(parts, axis=0)


def head_cols(h, offset=0):
    return slice(offset + h * HD, offset + (h + 1) * HD)


def scores_of(q_ref, kv_refs, bias):
    return [
        lax.dot_general(
            jnp.concatenate([r[:, head_cols(h)] for r in kv_refs], axis=0),
            q_ref[:, head_cols(h)],
            (((1,), (1,)), ((), ())),
            preferred_element_type=F32,
        )
        + bias
        for h in range(q_ref.shape[1] // HD)
    ]


def raised_from(scores, peaks):
    return [jnp.exp((s - peaks[h : h + 1]) * HD ** (-0.5)) for h, s in enumerate(scores)]


def reduced(reduce, per_head):
    return jnp.concatenate([reduce(x, axis=0, keepdims=True) for x in per_head], axis=0)


def mixes_of(kv_refs, raised):
    inner = kv_refs[0].shape[1] // 2
    return [
        lax.dot_general(
            jnp.concatenate([r[:, head_cols(h, inner)] for r in kv_refs], axis=0),
            x.astype(BF16),
            (((0,), (0,)), ((), ())),
            preferred_element_type=F32,
        )
        for h, x in enumerate(raised)
    ]


def near_kernel(n_kv, tile_len, slots_of, lists_ref, q_weight_ref, _, normed_ref, *refs):
    kv_refs = refs[:n_kv]
    q_ref, peak_ref, total_ref, mix_ref = refs[n_kv:]
    q_ref[...] = projected(normed_ref[...], q_weight_ref[...])
    count, key_count = normed_ref.shape[0], sum(r.shape[0] for r in kv_refs)
    bias = masking(lists_ref, slots_of(), tile_len, 0, key_count, count)
    scores = scores_of(q_ref, kv_refs, bias)
    peaks = reduced(jnp.max, scores)
    raised = raised_from(scores, peaks)
    peak_ref[...] = peaks
    total_ref[...] = reduced(jnp.sum, raised)
    for h, mix in enumerate(mixes_of(kv_refs, raised)):
        mix_ref[head_cols(h), :] = mix


def finish_kernel(
    n_kv, tile_len, slots_of, first,
    lists_ref, modulate_ref, out_weight_ref, rows_ref, q_ref, peak_ref, total_ref, mix_ref, *refs
):
    kv_refs, (mixed_ref, finished_ref) = refs[:n_kv], refs[n_kv:]
    count = rows_ref.shape[0]
    key_count = sum(r.shape[0] for r in kv_refs)
    bias = masking(lists_ref, slots_of(), tile_len, first, key_count, count)
    scores = scores_of(q_ref, kv_refs, bias)
    before = peak_ref[...]
    peaks = jnp.maximum(reduced(jnp.max, scores), before)
    raised = raised_from(scores, peaks)
    kept = jnp.exp((before - peaks) * HD ** (-0.5))
    share = 1.0 / (total_ref[...] * kept + reduced(jnp.sum, raised))
    kept = kept * share
    for h, mix in enumerate(mixes_of(kv_refs, raised)):
        mixed_ref[head_cols(h), :] = (
            mix_ref[head_cols(h), :] * kept[h : h + 1] + mix * share[h : h + 1]
        ).astype(BF16)
    output_columns(0, mixed_ref, modulate_ref, out_weight_ref, rows_ref, finished_ref)


def output_columns(first, mixed_ref, modulate_ref, out_weight_ref, rows_ref, finished_ref):
    cols = slice(first, first + finished_ref.shape[1])
    branch = lax.dot_general(
        mixed_ref[...],
        out_weight_ref[:, cols],
        (((0,), (0,)), ((), ())),
        preferred_element_type=F32,
    )
    finished_ref[...] = (
        rows_ref[:, cols].astype(F32) + modulate_ref[2:3, cols] * branch
    ).astype(BF16)


def swap_perm(size):
    return [(i, i ^ 1) for i in range(size)]


def relay_perm(size):
    return [(i, i + 2) for i in range(0, size - 2, 2)] + [(i, i - 2) for i in range(3, size, 2)]


def beyond_perm(size):
    return [((i + (2 if i % 2 == 0 else -2)) % size, i) for i in range(size)]


def in_hbm(x):
    return pltpu.with_memory_space_constraint(x, pltpu.HBM)


def after(x, *others):
    return lax.optimization_barrier((x, *others))[0]


def call(kernel, ins, outs, args, scratch=(), name=None, weight=1):
    return pl.pallas_call(
        kernel,
        out_shape=outs,
        in_specs=ins,
        out_specs=[VMEM] * len(outs),
        scratch_shapes=scratch,
        compiler_params=PARAMS,
        cost_estimate=pl.CostEstimate(flops=weight, bytes_accessed=0, transcendentals=0),
        name=name,
    )(*args)


def body(clip_tokens, qkv_weight, out_weight, modulation, domain_ids, tile_lists):
    col_tiles, tile_len, width = clip_tokens.shape[3:]
    own_count = col_tiles * tile_len
    inner = out_weight.shape[1]
    heads = inner // HD
    frames, rows = lax.axis_size("frame"), lax.axis_size("row")
    segments = lax.axis_size("segment")
    modulation_table = jnp.transpose(modulation[0], (1, 0, 2))
    weight = qkv_weight[0]
    own = clip_tokens.reshape(own_count, width)

    def held(count, wide, dtype=BF16):
        return pltpu.VMEM((count, wide), dtype)

    def from_partner(x):
        return lax.ppermute(x, "frame", swap_perm(frames))

    def from_beyond(x):
        return lax.ppermute(x, "frame", beyond_perm(frames))

    tokens = from_partner(own)
    lists = from_partner(tile_lists[0, 0])
    far = frames > 2
    sent = own_count * RAW // 8
    beyond = [from_beyond(own[:sent])] if far else []

    modulate, q_weight, pair_weight, kv_own, *tail = call(
        functools.partial(load_kernel, inner),
        [pl.BlockSpec(memory_space=pl.ANY)] + [HBM] * 3,
        [held(3, width, F32), held(width, inner), held(width, 2 * inner), held(own_count, 2 * inner)]
        + [held(own_count - sent, 2 * inner)] * far,
        [domain_ids, *map(in_hbm, (modulation_table, weight, own))],
        [
            pltpu.SMEM(domain_ids.shape, jnp.int32),
            pltpu.VMEM(modulation_table.shape, BF16),
            pltpu.VMEM((own_count, width), BF16),
            pltpu.SemaphoreType.DMA((4 + LOADS,)),
        ],
        "own_pairs",
    )
    kv_tail = [from_beyond(t) for t in tail]
    kv_beyond = [
        call(
            beyond_kernel,
            [VMEM] * 3,
            [held(sent, 2 * inner)],
            [modulate, pair_weight, b],
            name="beyond_pairs",
        )[0]
        for b in beyond
    ]
    near_tiles = 2 + far

    def slots_of():
        odd_frame = 1 - lax.axis_index("frame") % 2
        odd_row = lax.axis_index("row") % 2
        return [
            0,
            2 - odd_frame,
            1 + odd_frame,
            near_tiles + 1 - odd_row,
            near_tiles + odd_row,
        ]

    tokens = after(tokens, kv_own, *kv_beyond)
    kv_tokens, normed = call(
        pair_kernel,
        [VMEM] * 3,
        [held(own_count, 2 * inner), held(own_count, width)],
        [modulate, pair_weight, tokens],
        name="pairs",
    )
    kv_rows = [lax.ppermute(kv_tokens, "row", swap_perm(rows))]
    if rows > 2:
        kv_rows.append(lax.ppermute(kv_rows[0], "row", relay_perm(rows)))
    near = [kv_tokens, kv_own]
    q, *partial = call(
        functools.partial(near_kernel, len(near), tile_len, slots_of),
        [VMEM] * (4 + len(near)),
        [
            held(own_count, inner),
            held(heads, own_count, F32),
            held(heads, own_count, F32),
            held(inner, own_count, F32),
        ],
        [lists, q_weight, out_weight[0], normed, *near],
        name="near_attention",
        weight=10**10,
    )
    late = [*kv_beyond, *kv_tail, *kv_rows]
    first_cols = width * FIRST // 12
    mixed, *finished = call(
        functools.partial(
            finish_kernel, len(late), tile_len, slots_of, sum(x.shape[0] for x in near)
        ),
        [VMEM] * (8 + len(late)),
        [held(inner, own_count), held(own_count, first_cols)],
        [lists, modulate, out_weight[0], tokens, q, *partial, *late],
        name="finish",
    )
    finished += call(
        functools.partial(output_columns, first_cols),
        [VMEM] * 4,
        [held(own_count, width - first_cols)],
        [mixed, modulate, out_weight[0], tokens],
        name="finish_rest",
    )
    onward = [
        (s * frames + f, (s + 1) % segments * frames + (f ^ 1))
        for s in range(segments)
        for f in range(frames)
    ]
    handed = [lax.ppermute(x, ("segment", "frame"), onward) for x in finished]
    return jnp.concatenate(handed, axis=1).reshape(clip_tokens.shape)


def solution(mesh):
    return jax.shard_map(
        body,
        mesh=mesh,
        in_specs=(
            P("segment", "frame", "row", None, None, None),
            P("segment", None, None),
            P("segment", None, None),
            P("segment", None, None, None),
            P("segment"),
            P("frame", "row", None, None),
        ),
        out_specs=P("segment", "frame", "row", None, None, None),
        check_vma=False,
    )
```

```python
import functools

import jax
import jax.numpy as jnp
from jax import lax
from jax.experimental import pallas as pl
from jax.experimental.pallas import tpu as pltpu
from jax.sharding import PartitionSpec as P

HD = 128
EPSILON = 1e-06
MASKED = -1e30
RAW = 5
LOADS = 4
FIRST = 7
F32 = jnp.float32
BF16 = jnp.bfloat16
VMEM = pl.BlockSpec(memory_space=pltpu.VMEM)
SMEM = pl.BlockSpec(memory_space=pltpu.SMEM)
HBM = pl.BlockSpec(memory_space=pltpu.HBM)
PARAMS = pltpu.CompilerParams(vmem_limit_bytes=32 * 1024 * 1024)


def modulate_rows(domain_ref, modulation_ref):
    table = modulation_ref[...].astype(F32)
    row = lax.broadcasted_iota(jnp.int32, table.shape, 1)
    return jnp.sum(jnp.where(row == domain_ref[0], table, 0.0), axis=1)


def normalize(rows, shift, scale):
    values = rows.astype(F32)
    centered = values - jnp.mean(values, axis=-1, keepdims=True)
    row_var = jnp.mean(centered * centered, axis=-1, keepdims=True)
    return (centered * lax.rsqrt(row_var + EPSILON) * (1.0 + scale) + shift).astype(BF16)


def normalized(refs, modulate_ref):
    shift, scale = modulate_ref[0:1, :], modulate_ref[1:2, :]
    return jnp.concatenate([normalize(r[...], shift, scale) for r in refs], axis=0)


def projected(rows, weight):
    return jnp.dot(rows, weight, preferred_element_type=F32).astype(BF16)


def load_kernel(
    inner, domain_hbm, modulation_hbm, weight_hbm, own_hbm,
    modulate_ref, q_weight_ref, weight_ref, kv_ref, *refs
):
    *tail_ref, domain_ref, modulation_ref, own_ref, sems = refs
    first = [
        pltpu.make_async_copy(domain_hbm, domain_ref, sems.at[0]),
        pltpu.make_async_copy(modulation_hbm, modulation_ref, sems.at[1]),
        pltpu.make_async_copy(own_hbm, own_ref, sems.at[2]),
    ]
    part = 2 * inner // LOADS
    loads = [
        pltpu.make_async_copy(
            weight_hbm.at[:, pl.ds(inner + i * part, part)],
            weight_ref.at[:, pl.ds(i * part, part)],
            sems.at[3 + i],
        )
        for i in range(LOADS)
    ]
    query = pltpu.make_async_copy(weight_hbm.at[:, pl.ds(0, inner)], q_weight_ref, sems.at[3 + LOADS])
    for load in first + loads + [query]:
        load.start()
    for load in first:
        load.wait()
    modulate_ref[...] = modulate_rows(domain_ref, modulation_ref)
    rows = normalized((own_ref,), modulate_ref)
    for i, load in enumerate(loads):
        load.wait()
        cols = slice(i * part, (i + 1) * part)
        pairs = projected(rows, weight_ref[:, cols])
        kv_ref[:, cols] = pairs
        for ref in tail_ref:
            ref[:, cols] = pairs[rows.shape[0] - ref.shape[0] :]
    query.wait()


def beyond_kernel(modulate_ref, weight_ref, rows_ref, kv_ref):
    kv_ref[...] = projected(normalized((rows_ref,), modulate_ref), weight_ref[...])


def pair_kernel(modulate_ref, weight_ref, rows_ref, kv_ref, normed_ref):
    rows = normalized((rows_ref,), modulate_ref)
    normed_ref[...] = rows
    kv_ref[...] = projected(rows, weight_ref[...])


def masking(lists_ref, slots, tile_len, first, key_count, query_count):
    col_tiles = query_count // tile_len
    numbers = lists_ref[...]
    slot = jnp.full(numbers.shape, slots[0], jnp.int32)
    for d in range(1, 5):
        slot = jnp.where(numbers // col_tiles == d, slots[d], slot)
    bits = jnp.sum(
        jnp.int32(1) << (slot * col_tiles + numbers % col_tiles), axis=1, keepdims=True
    )
    tile = lax.broadcasted_iota(jnp.int32, (1, query_count), 1) // tile_len
    row = jnp.zeros((1, query_count), jnp.int32)
    for t in range(col_tiles):
        row = jnp.where(tile == t, bits[t : t + 1, :], row)
    parts, end = [], first + key_count
    for p in range(first // tile_len, pl.cdiv(end, tile_len)):
        size = min(end, (p + 1) * tile_len) - max(first, p * tile_len)
        added = jnp.where((row >> p) & 1 == 1, 0.0, MASKED)
        parts.append(jnp.broadcast_to(added, (size, query_count)))
    return jnp.concatenate(parts, axis=0)


def head_cols(h, offset=0):
    return slice(offset + h * HD, offset + (h + 1) * HD)


def scores_of(q_ref, kv_refs, bias):
    return [
        lax.dot_general(
            jnp.concatenate([r[:, head_cols(h)] for r in kv_refs], axis=0),
            q_ref[:, head_cols(h)],
            (((1,), (1,)), ((), ())),
            preferred_element_type=F32,
        )
        + bias
        for h in range(q_ref.shape[1] // HD)
    ]


def raised_from(scores, peaks):
    return [jnp.exp((s - peaks[h : h + 1]) * HD ** (-0.5)) for h, s in enumerate(scores)]


def reduced(reduce, per_head):
    return jnp.concatenate([reduce(x, axis=0, keepdims=True) for x in per_head], axis=0)


def mixes_of(kv_refs, raised):
    inner = kv_refs[0].shape[1] // 2
    return [
        lax.dot_general(
            jnp.concatenate([r[:, head_cols(h, inner)] for r in kv_refs], axis=0),
            x.astype(BF16),
            (((0,), (0,)), ((), ())),
            preferred_element_type=F32,
        )
        for h, x in enumerate(raised)
    ]


def near_kernel(n_kv, tile_len, slots_of, lists_ref, q_weight_ref, _, normed_ref, *refs):
    kv_refs = refs[:n_kv]
    q_ref, peak_ref, total_ref, mix_ref = refs[n_kv:]
    q_ref[...] = projected(normed_ref[...], q_weight_ref[...])
    count, key_count = normed_ref.shape[0], sum(r.shape[0] for r in kv_refs)
    bias = masking(lists_ref, slots_of(), tile_len, 0, key_count, count)
    scores = scores_of(q_ref, kv_refs, bias)
    peaks = reduced(jnp.max, scores)
    raised = raised_from(scores, peaks)
    peak_ref[...] = peaks
    total_ref[...] = reduced(jnp.sum, raised)
    for h, mix in enumerate(mixes_of(kv_refs, raised)):
        mix_ref[head_cols(h), :] = mix


def finish_kernel(
    n_kv, tile_len, slots_of, first,
    lists_ref, modulate_ref, out_weight_ref, rows_ref, q_ref, peak_ref, total_ref, mix_ref, *refs
):
    kv_refs, (mixed_ref, finished_ref) = refs[:n_kv], refs[n_kv:]
    count = rows_ref.shape[0]
    key_count = sum(r.shape[0] for r in kv_refs)
    bias = masking(lists_ref, slots_of(), tile_len, first, key_count, count)
    scores = scores_of(q_ref, kv_refs, bias)
    before = peak_ref[...]
    peaks = jnp.maximum(reduced(jnp.max, scores), before)
    raised = raised_from(scores, peaks)
    kept = jnp.exp((before - peaks) * HD ** (-0.5))
    share = 1.0 / (total_ref[...] * kept + reduced(jnp.sum, raised))
    kept = kept * share
    for h, mix in enumerate(mixes_of(kv_refs, raised)):
        mixed_ref[head_cols(h), :] = (
            mix_ref[head_cols(h), :] * kept[h : h + 1] + mix * share[h : h + 1]
        ).astype(BF16)
    output_columns(0, mixed_ref, modulate_ref, out_weight_ref, rows_ref, finished_ref)


def output_columns(first, mixed_ref, modulate_ref, out_weight_ref, rows_ref, finished_ref):
    cols = slice(first, first + finished_ref.shape[1])
    branch = lax.dot_general(
        mixed_ref[...],
        out_weight_ref[:, cols],
        (((0,), (0,)), ((), ())),
        preferred_element_type=F32,
    )
    finished_ref[...] = (
        rows_ref[:, cols].astype(F32) + modulate_ref[2:3, cols] * branch
    ).astype(BF16)


def first_kernel(part_ref, whole_hbm, sem):
    copy = pltpu.make_async_copy(part_ref, whole_hbm.at[:, pl.ds(0, part_ref.shape[1])], sem)
    copy.start()
    copy.wait()


def rest_kernel(_, part_ref, whole_hbm, sem):
    first = whole_hbm.shape[1] - part_ref.shape[1]
    copy = pltpu.make_async_copy(part_ref, whole_hbm.at[:, pl.ds(first, part_ref.shape[1])], sem)
    copy.start()
    copy.wait()


def swap_perm(size):
    return [(i, i ^ 1) for i in range(size)]


def relay_perm(size):
    return [(i, i + 2) for i in range(0, size - 2, 2)] + [(i, i - 2) for i in range(3, size, 2)]


def beyond_perm(size):
    return [((i + (2 if i % 2 == 0 else -2)) % size, i) for i in range(size)]


def in_hbm(x):
    return pltpu.with_memory_space_constraint(x, pltpu.HBM)


def after(x, *others):
    return lax.optimization_barrier((x, *others))[0]


def call(kernel, ins, outs, args, scratch=(), name=None, weight=1):
    return pl.pallas_call(
        kernel,
        out_shape=outs,
        in_specs=ins,
        out_specs=[VMEM] * len(outs),
        scratch_shapes=scratch,
        compiler_params=PARAMS,
        cost_estimate=pl.CostEstimate(flops=weight, bytes_accessed=0, transcendentals=0),
        name=name,
    )(*args)


def body(clip_tokens, qkv_weight, out_weight, modulation, domain_ids, tile_lists):
    col_tiles, tile_len, width = clip_tokens.shape[3:]
    own_count = col_tiles * tile_len
    inner = out_weight.shape[1]
    heads = inner // HD
    frames, rows = lax.axis_size("frame"), lax.axis_size("row")
    segments = lax.axis_size("segment")
    modulation_table = jnp.transpose(modulation[0], (1, 0, 2))
    weight = qkv_weight[0]
    own = clip_tokens.reshape(own_count, width)

    def held(count, wide, dtype=BF16):
        return pltpu.VMEM((count, wide), dtype)

    def from_partner(x):
        return lax.ppermute(x, "frame", swap_perm(frames))

    def from_beyond(x):
        return lax.ppermute(x, "frame", beyond_perm(frames))

    tokens = from_partner(own)
    lists = from_partner(tile_lists[0, 0])
    far = frames > 2
    sent = own_count * RAW // 8
    beyond = [from_beyond(own[:sent])] if far else []

    modulate, q_weight, pair_weight, kv_own, *tail = call(
        functools.partial(load_kernel, inner),
        [pl.BlockSpec(memory_space=pl.ANY)] + [HBM] * 3,
        [held(3, width, F32), held(width, inner), held(width, 2 * inner), held(own_count, 2 * inner)]
        + [held(own_count - sent, 2 * inner)] * far,
        [domain_ids, *map(in_hbm, (modulation_table, weight, own))],
        [
            pltpu.SMEM(domain_ids.shape, jnp.int32),
            pltpu.VMEM(modulation_table.shape, BF16),
            pltpu.VMEM((own_count, width), BF16),
            pltpu.SemaphoreType.DMA((4 + LOADS,)),
        ],
        "own_pairs",
    )
    kv_tail = [from_beyond(t) for t in tail]
    kv_beyond = [
        call(
            beyond_kernel,
            [VMEM] * 3,
            [held(sent, 2 * inner)],
            [modulate, pair_weight, b],
            name="beyond_pairs",
        )[0]
        for b in beyond
    ]
    near_tiles = 2 + far

    def slots_of():
        odd_frame = 1 - lax.axis_index("frame") % 2
        odd_row = lax.axis_index("row") % 2
        return [
            0,
            2 - odd_frame,
            1 + odd_frame,
            near_tiles + 1 - odd_row,
            near_tiles + odd_row,
        ]

    tokens = after(tokens, kv_own, *kv_beyond)
    kv_tokens, normed = call(
        pair_kernel,
        [VMEM] * 3,
        [held(own_count, 2 * inner), held(own_count, width)],
        [modulate, pair_weight, tokens],
        name="pairs",
    )
    kv_rows = [lax.ppermute(kv_tokens, "row", swap_perm(rows))]
    if rows > 2:
        kv_rows.append(lax.ppermute(kv_rows[0], "row", relay_perm(rows)))
    near = [kv_tokens, kv_own]
    q, *partial = call(
        functools.partial(near_kernel, len(near), tile_len, slots_of),
        [VMEM] * (4 + len(near)),
        [
            held(own_count, inner),
            held(heads, own_count, F32),
            held(heads, own_count, F32),
            held(inner, own_count, F32),
        ],
        [lists, q_weight, out_weight[0], normed, *near],
        name="near_attention",
        weight=10**10,
    )
    late = [*kv_beyond, *kv_tail, *kv_rows]
    first_cols = width * FIRST // 12
    mixed, *finished = call(
        functools.partial(
            finish_kernel, len(late), tile_len, slots_of, sum(x.shape[0] for x in near)
        ),
        [VMEM] * (8 + len(late)),
        [held(inner, own_count), held(own_count, first_cols)],
        [lists, modulate, out_weight[0], tokens, q, *partial, *late],
        name="finish",
    )
    finished += call(
        functools.partial(output_columns, first_cols),
        [VMEM] * 4,
        [held(own_count, width - first_cols)],
        [mixed, modulate, out_weight[0], tokens],
        name="finish_rest",
    )
    onward = [
        (s * frames + f, (s + 1) % segments * frames + (f ^ 1))
        for s in range(segments)
        for f in range(frames)
    ]
    handed = [lax.ppermute(x, ("segment", "frame"), onward) for x in finished]
    result = jax.ShapeDtypeStruct((own_count, width), BF16)
    out = pl.pallas_call(
        first_kernel,
        out_shape=result,
        in_specs=[VMEM],
        out_specs=HBM,
        scratch_shapes=[pltpu.SemaphoreType.DMA],
        compiler_params=PARAMS,
        name="first_columns",
    )(handed[0])
    out = pl.pallas_call(
        rest_kernel,
        out_shape=result,
        in_specs=[HBM, VMEM],
        out_specs=HBM,
        scratch_shapes=[pltpu.SemaphoreType.DMA],
        input_output_aliases={0: 0},
        compiler_params=PARAMS,
        name="other_columns",
    )(out, handed[1])
    return out.reshape(clip_tokens.shape)


def solution(mesh):
    return jax.shard_map(
        body,
        mesh=mesh,
        in_specs=(
            P("segment", "frame", "row", None, None, None),
            P("segment", None, None),
            P("segment", None, None),
            P("segment", None, None, None),
            P("segment"),
            P("frame", "row", None, None),
        ),
        out_specs=P("segment", "frame", "row", None, None, None),
        check_vma=False,
    )
```

```python
import functools

import jax
import jax.numpy as jnp
from jax import lax
from jax.experimental import pallas as pl
from jax.experimental.pallas import tpu as pltpu
from jax.sharding import PartitionSpec as P

HD = 128
EPSILON = 1e-06
MASKED = -1e30
RAW = 5
LOADS = 4
FIRST = 7
F32 = jnp.float32
BF16 = jnp.bfloat16
VMEM = pl.BlockSpec(memory_space=pltpu.VMEM)
SMEM = pl.BlockSpec(memory_space=pltpu.SMEM)
HBM = pl.BlockSpec(memory_space=pltpu.HBM)
PARAMS = pltpu.CompilerParams(vmem_limit_bytes=32 * 1024 * 1024)


def modulate_rows(domain_ref, modulation_ref):
    table = modulation_ref[...].astype(F32)
    row = lax.broadcasted_iota(jnp.int32, table.shape, 1)
    return jnp.sum(jnp.where(row == domain_ref[0], table, 0.0), axis=1)


def normalize(rows, shift, scale):
    values = rows.astype(F32)
    centered = values - jnp.mean(values, axis=-1, keepdims=True)
    row_var = jnp.mean(centered * centered, axis=-1, keepdims=True)
    return (centered * lax.rsqrt(row_var + EPSILON) * (1.0 + scale) + shift).astype(BF16)


def normalized(refs, modulate_ref):
    shift, scale = modulate_ref[0:1, :], modulate_ref[1:2, :]
    return jnp.concatenate([normalize(r[...], shift, scale) for r in refs], axis=0)


def projected(rows, weight):
    return jnp.dot(rows, weight, preferred_element_type=F32).astype(BF16)


def load_kernel(
    inner, domain_hbm, modulation_hbm, weight_hbm, own_hbm,
    modulate_ref, q_weight_ref, weight_ref, kv_ref, *refs
):
    *tail_ref, domain_ref, modulation_ref, own_ref, sems = refs
    first = [
        pltpu.make_async_copy(domain_hbm, domain_ref, sems.at[0]),
        pltpu.make_async_copy(modulation_hbm, modulation_ref, sems.at[1]),
        pltpu.make_async_copy(own_hbm, own_ref, sems.at[2]),
    ]
    part = 2 * inner // LOADS
    loads = [
        pltpu.make_async_copy(
            weight_hbm.at[:, pl.ds(inner + i * part, part)],
            weight_ref.at[:, pl.ds(i * part, part)],
            sems.at[3 + i],
        )
        for i in range(LOADS)
    ]
    query = pltpu.make_async_copy(weight_hbm.at[:, pl.ds(0, inner)], q_weight_ref, sems.at[3 + LOADS])
    for load in first + loads + [query]:
        load.start()
    for load in first:
        load.wait()
    modulate_ref[...] = modulate_rows(domain_ref, modulation_ref)
    rows = normalized((own_ref,), modulate_ref)
    for i, load in enumerate(loads):
        load.wait()
        cols = slice(i * part, (i + 1) * part)
        pairs = projected(rows, weight_ref[:, cols])
        kv_ref[:, cols] = pairs
        for ref in tail_ref:
            ref[:, cols] = pairs[rows.shape[0] - ref.shape[0] :]
    query.wait()


def beyond_kernel(modulate_ref, weight_ref, rows_ref, kv_ref):
    kv_ref[...] = projected(normalized((rows_ref,), modulate_ref), weight_ref[...])


def pair_kernel(modulate_ref, weight_ref, rows_ref, kv_ref, normed_ref):
    rows = normalized((rows_ref,), modulate_ref)
    normed_ref[...] = rows
    kv_ref[...] = projected(rows, weight_ref[...])


def masking(lists_ref, slots, tile_len, first, key_count, query_count):
    col_tiles = query_count // tile_len
    numbers = lists_ref[...]
    slot = jnp.full(numbers.shape, slots[0], jnp.int32)
    for d in range(1, 5):
        slot = jnp.where(numbers // col_tiles == d, slots[d], slot)
    bits = jnp.sum(
        jnp.int32(1) << (slot * col_tiles + numbers % col_tiles), axis=1, keepdims=True
    )
    tile = lax.broadcasted_iota(jnp.int32, (1, query_count), 1) // tile_len
    row = jnp.zeros((1, query_count), jnp.int32)
    for t in range(col_tiles):
        row = jnp.where(tile == t, bits[t : t + 1, :], row)
    parts, end = [], first + key_count
    for p in range(first // tile_len, pl.cdiv(end, tile_len)):
        size = min(end, (p + 1) * tile_len) - max(first, p * tile_len)
        added = jnp.where((row >> p) & 1 == 1, 0.0, MASKED)
        parts.append(jnp.broadcast_to(added, (size, query_count)))
    return jnp.concatenate(parts, axis=0)


def head_cols(h, offset=0):
    return slice(offset + h * HD, offset + (h + 1) * HD)


def scores_of(q_ref, kv_refs, bias):
    return [
        lax.dot_general(
            jnp.concatenate([r[:, head_cols(h)] for r in kv_refs], axis=0),
            q_ref[:, head_cols(h)],
            (((1,), (1,)), ((), ())),
            preferred_element_type=F32,
        )
        + bias
        for h in range(q_ref.shape[1] // HD)
    ]


def raised_from(scores, peaks):
    return [jnp.exp((s - peaks[h : h + 1]) * HD ** (-0.5)) for h, s in enumerate(scores)]


def reduced(reduce, per_head):
    return jnp.concatenate([reduce(x, axis=0, keepdims=True) for x in per_head], axis=0)


def mixes_of(kv_refs, raised):
    inner = kv_refs[0].shape[1] // 2
    return [
        lax.dot_general(
            jnp.concatenate([r[:, head_cols(h, inner)] for r in kv_refs], axis=0),
            x.astype(BF16),
            (((0,), (0,)), ((), ())),
            preferred_element_type=F32,
        )
        for h, x in enumerate(raised)
    ]


def near_kernel(n_kv, tile_len, slots_of, lists_ref, q_weight_ref, _, normed_ref, *refs):
    kv_refs = refs[:n_kv]
    q_ref, peak_ref, total_ref, mix_ref = refs[n_kv:]
    q_ref[...] = projected(normed_ref[...], q_weight_ref[...])
    count, key_count = normed_ref.shape[0], sum(r.shape[0] for r in kv_refs)
    bias = masking(lists_ref, slots_of(), tile_len, 0, key_count, count)
    scores = scores_of(q_ref, kv_refs, bias)
    peaks = reduced(jnp.max, scores)
    raised = raised_from(scores, peaks)
    peak_ref[...] = peaks
    total_ref[...] = reduced(jnp.sum, raised)
    for h, mix in enumerate(mixes_of(kv_refs, raised)):
        mix_ref[head_cols(h), :] = mix


def finish_kernel(
    n_far, n_kv, tile_len, slots_of, has_far, first,
    lists_ref, modulate_ref, out_weight_ref, rows_ref, q_ref, peak_ref, total_ref, mix_ref, *refs
):
    mixed_ref, finished_ref = refs[n_kv:]

    def join(kv_refs, first):
        key_count = sum(r.shape[0] for r in kv_refs)
        bias = masking(lists_ref, slots_of(), tile_len, first, key_count, rows_ref.shape[0])
        scores = scores_of(q_ref, kv_refs, bias)
        before = peak_ref[...]
        peaks = jnp.maximum(reduced(jnp.max, scores), before)
        raised = raised_from(scores, peaks)
        kept = jnp.exp((before - peaks) * HD ** (-0.5))
        share = 1.0 / (total_ref[...] * kept + reduced(jnp.sum, raised))
        kept = kept * share
        for h, mix in enumerate(mixes_of(kv_refs, raised)):
            mixed_ref[head_cols(h), :] = (
                mix_ref[head_cols(h), :] * kept[h : h + 1] + mix * share[h : h + 1]
            ).astype(BF16)

    if n_far:
        far = has_far()

        @pl.when(far)
        def _():
            join(refs[:n_kv], first)

        @pl.when(jnp.logical_not(far))
        def _():
            join(refs[n_far:n_kv], first + sum(r.shape[0] for r in refs[:n_far]))

    else:
        join(refs[:n_kv], first)
    output_columns(0, mixed_ref, modulate_ref, out_weight_ref, rows_ref, finished_ref)


def output_columns(first, mixed_ref, modulate_ref, out_weight_ref, rows_ref, finished_ref):
    cols = slice(first, first + finished_ref.shape[1])
    branch = lax.dot_general(
        mixed_ref[...],
        out_weight_ref[:, cols],
        (((0,), (0,)), ((), ())),
        preferred_element_type=F32,
    )
    finished_ref[...] = (
        rows_ref[:, cols].astype(F32) + modulate_ref[2:3, cols] * branch
    ).astype(BF16)


def first_kernel(part_ref, whole_hbm, sem):
    copy = pltpu.make_async_copy(part_ref, whole_hbm.at[:, pl.ds(0, part_ref.shape[1])], sem)
    copy.start()
    copy.wait()


def rest_kernel(_, part_ref, whole_hbm, sem):
    first = whole_hbm.shape[1] - part_ref.shape[1]
    copy = pltpu.make_async_copy(part_ref, whole_hbm.at[:, pl.ds(first, part_ref.shape[1])], sem)
    copy.start()
    copy.wait()


def swap_perm(size):
    return [(i, i ^ 1) for i in range(size)]


def relay_perm(size):
    return [(i, i + 2) for i in range(0, size - 2, 2)] + [(i, i - 2) for i in range(3, size, 2)]


def beyond_perm(size):
    return [((i + (2 if i % 2 == 0 else -2)) % size, i) for i in range(size)]


def in_hbm(x):
    return pltpu.with_memory_space_constraint(x, pltpu.HBM)


def after(x, *others):
    return lax.optimization_barrier((x, *others))[0]


def call(kernel, ins, outs, args, scratch=(), name=None, weight=1):
    return pl.pallas_call(
        kernel,
        out_shape=outs,
        in_specs=ins,
        out_specs=[VMEM] * len(outs),
        scratch_shapes=scratch,
        compiler_params=PARAMS,
        cost_estimate=pl.CostEstimate(flops=weight, bytes_accessed=0, transcendentals=0),
        name=name,
    )(*args)


def body(clip_tokens, qkv_weight, out_weight, modulation, domain_ids, tile_lists):
    col_tiles, tile_len, width = clip_tokens.shape[3:]
    own_count = col_tiles * tile_len
    inner = out_weight.shape[1]
    heads = inner // HD
    frames, rows = lax.axis_size("frame"), lax.axis_size("row")
    segments = lax.axis_size("segment")
    modulation_table = jnp.transpose(modulation[0], (1, 0, 2))
    weight = qkv_weight[0]
    own = clip_tokens.reshape(own_count, width)

    def held(count, wide, dtype=BF16):
        return pltpu.VMEM((count, wide), dtype)

    def from_partner(x):
        return lax.ppermute(x, "frame", swap_perm(frames))

    def from_beyond(x):
        return lax.ppermute(x, "frame", beyond_perm(frames))

    tokens = from_partner(own)
    lists = from_partner(tile_lists[0, 0])
    far = frames > 2
    sent = own_count * RAW // 8
    beyond = [from_beyond(own[:sent])] if far else []

    modulate, q_weight, pair_weight, kv_own, *tail = call(
        functools.partial(load_kernel, inner),
        [pl.BlockSpec(memory_space=pl.ANY)] + [HBM] * 3,
        [held(3, width, F32), held(width, inner), held(width, 2 * inner), held(own_count, 2 * inner)]
        + [held(own_count - sent, 2 * inner)] * far,
        [domain_ids, *map(in_hbm, (modulation_table, weight, own))],
        [
            pltpu.SMEM(domain_ids.shape, jnp.int32),
            pltpu.VMEM(modulation_table.shape, BF16),
            pltpu.VMEM((own_count, width), BF16),
            pltpu.SemaphoreType.DMA((4 + LOADS,)),
        ],
        "own_pairs",
    )
    kv_tail = [from_beyond(t) for t in tail]
    kv_beyond = [
        call(
            beyond_kernel,
            [VMEM] * 3,
            [held(sent, 2 * inner)],
            [modulate, pair_weight, b],
            name="beyond_pairs",
        )[0]
        for b in beyond
    ]
    near_tiles = 2 + far

    def slots_of():
        odd_frame = 1 - lax.axis_index("frame") % 2
        odd_row = lax.axis_index("row") % 2
        return [
            0,
            2 - odd_frame,
            1 + odd_frame,
            near_tiles + 1 - odd_row,
            near_tiles + odd_row,
        ]

    tokens = after(tokens, kv_own, *kv_beyond)
    kv_tokens, normed = call(
        pair_kernel,
        [VMEM] * 3,
        [held(own_count, 2 * inner), held(own_count, width)],
        [modulate, pair_weight, tokens],
        name="pairs",
    )
    kv_rows = [lax.ppermute(kv_tokens, "row", swap_perm(rows))]
    if rows > 2:
        kv_rows.append(lax.ppermute(kv_rows[0], "row", relay_perm(rows)))
    near = [kv_tokens, kv_own]
    q, *partial = call(
        functools.partial(near_kernel, len(near), tile_len, slots_of),
        [VMEM] * (4 + len(near)),
        [
            held(own_count, inner),
            held(heads, own_count, F32),
            held(heads, own_count, F32),
            held(inner, own_count, F32),
        ],
        [lists, q_weight, out_weight[0], normed, *near],
        name="near_attention",
        weight=10**10,
    )
    def has_far():
        frame = lax.axis_index("frame")
        return jnp.where(frame % 2 == 0, frame + 2 < frames, frame >= 2)

    late = [*kv_beyond, *kv_tail, *kv_rows]
    first_cols = width * FIRST // 12
    mixed, *finished = call(
        functools.partial(
            finish_kernel,
            len(late) - len(kv_rows),
            len(late),
            tile_len,
            slots_of,
            has_far,
            sum(x.shape[0] for x in near),
        ),
        [VMEM] * (8 + len(late)),
        [held(inner, own_count), held(own_count, first_cols)],
        [lists, modulate, out_weight[0], tokens, q, *partial, *late],
        name="finish",
    )
    finished += call(
        functools.partial(output_columns, first_cols),
        [VMEM] * 4,
        [held(own_count, width - first_cols)],
        [mixed, modulate, out_weight[0], tokens],
        name="finish_rest",
    )
    onward = [
        (s * frames + f, (s + 1) % segments * frames + (f ^ 1))
        for s in range(segments)
        for f in range(frames)
    ]
    handed = [lax.ppermute(x, ("segment", "frame"), onward) for x in finished]
    result = jax.ShapeDtypeStruct((own_count, width), BF16)
    out = pl.pallas_call(
        first_kernel,
        out_shape=result,
        in_specs=[VMEM],
        out_specs=HBM,
        scratch_shapes=[pltpu.SemaphoreType.DMA],
        compiler_params=PARAMS,
        name="first_columns",
    )(handed[0])
    out = pl.pallas_call(
        rest_kernel,
        out_shape=result,
        in_specs=[HBM, VMEM],
        out_specs=HBM,
        scratch_shapes=[pltpu.SemaphoreType.DMA],
        input_output_aliases={0: 0},
        compiler_params=PARAMS,
        name="other_columns",
    )(out, handed[1])
    return out.reshape(clip_tokens.shape)


def solution(mesh):
    return jax.shard_map(
        body,
        mesh=mesh,
        in_specs=(
            P("segment", "frame", "row", None, None, None),
            P("segment", None, None),
            P("segment", None, None),
            P("segment", None, None, None),
            P("segment"),
            P("frame", "row", None, None),
        ),
        out_specs=P("segment", "frame", "row", None, None, None),
        check_vma=False,
    )
```

```python
import functools

import jax
import jax.numpy as jnp
from jax import lax
from jax.experimental import pallas as pl
from jax.experimental.pallas import tpu as pltpu
from jax.sharding import PartitionSpec as P

HD = 128
EPSILON = 1e-06
MASKED = -1e30
RAW = 5
LOADS = 4
PARTS = (5, 4, 3)
F32 = jnp.float32
BF16 = jnp.bfloat16
VMEM = pl.BlockSpec(memory_space=pltpu.VMEM)
SMEM = pl.BlockSpec(memory_space=pltpu.SMEM)
HBM = pl.BlockSpec(memory_space=pltpu.HBM)
PARAMS = pltpu.CompilerParams(vmem_limit_bytes=32 * 1024 * 1024)


def modulate_rows(domain_ref, modulation_ref):
    table = modulation_ref[...].astype(F32)
    row = lax.broadcasted_iota(jnp.int32, table.shape, 1)
    return jnp.sum(jnp.where(row == domain_ref[0], table, 0.0), axis=1)


def normalize(rows, shift, scale):
    values = rows.astype(F32)
    centered = values - jnp.mean(values, axis=-1, keepdims=True)
    row_var = jnp.mean(centered * centered, axis=-1, keepdims=True)
    return (centered * lax.rsqrt(row_var + EPSILON) * (1.0 + scale) + shift).astype(BF16)


def normalized(refs, modulate_ref):
    shift, scale = modulate_ref[0:1, :], modulate_ref[1:2, :]
    return jnp.concatenate([normalize(r[...], shift, scale) for r in refs], axis=0)


def projected(rows, weight):
    return jnp.dot(rows, weight, preferred_element_type=F32).astype(BF16)


def load_kernel(
    inner, domain_hbm, modulation_hbm, weight_hbm, own_hbm,
    modulate_ref, q_weight_ref, weight_ref, kv_ref, *refs
):
    *tail_ref, domain_ref, modulation_ref, own_ref, sems = refs
    first = [
        pltpu.make_async_copy(domain_hbm, domain_ref, sems.at[0]),
        pltpu.make_async_copy(modulation_hbm, modulation_ref, sems.at[1]),
        pltpu.make_async_copy(own_hbm, own_ref, sems.at[2]),
    ]
    part = 2 * inner // LOADS
    loads = [
        pltpu.make_async_copy(
            weight_hbm.at[:, pl.ds(inner + i * part, part)],
            weight_ref.at[:, pl.ds(i * part, part)],
            sems.at[3 + i],
        )
        for i in range(LOADS)
    ]
    query = pltpu.make_async_copy(weight_hbm.at[:, pl.ds(0, inner)], q_weight_ref, sems.at[3 + LOADS])
    for load in first + loads + [query]:
        load.start()
    for load in first:
        load.wait()
    modulate_ref[...] = modulate_rows(domain_ref, modulation_ref)
    rows = normalized((own_ref,), modulate_ref)
    for i, load in enumerate(loads):
        load.wait()
        cols = slice(i * part, (i + 1) * part)
        pairs = projected(rows, weight_ref[:, cols])
        kv_ref[:, cols] = pairs
        for ref in tail_ref:
            ref[:, cols] = pairs[rows.shape[0] - ref.shape[0] :]
    query.wait()


def beyond_kernel(modulate_ref, weight_ref, rows_ref, kv_ref):
    kv_ref[...] = projected(normalized((rows_ref,), modulate_ref), weight_ref[...])


def pair_kernel(modulate_ref, weight_ref, rows_ref, kv_ref, normed_ref):
    rows = normalized((rows_ref,), modulate_ref)
    normed_ref[...] = rows
    kv_ref[...] = projected(rows, weight_ref[...])


def masking(lists_ref, slots, tile_len, first, key_count, query_count):
    col_tiles = query_count // tile_len
    numbers = lists_ref[...]
    slot = jnp.full(numbers.shape, slots[0], jnp.int32)
    for d in range(1, 5):
        slot = jnp.where(numbers // col_tiles == d, slots[d], slot)
    bits = jnp.sum(
        jnp.int32(1) << (slot * col_tiles + numbers % col_tiles), axis=1, keepdims=True
    )
    tile = lax.broadcasted_iota(jnp.int32, (1, query_count), 1) // tile_len
    row = jnp.zeros((1, query_count), jnp.int32)
    for t in range(col_tiles):
        row = jnp.where(tile == t, bits[t : t + 1, :], row)
    parts, end = [], first + key_count
    for p in range(first // tile_len, pl.cdiv(end, tile_len)):
        size = min(end, (p + 1) * tile_len) - max(first, p * tile_len)
        added = jnp.where((row >> p) & 1 == 1, 0.0, MASKED)
        parts.append(jnp.broadcast_to(added, (size, query_count)))
    return jnp.concatenate(parts, axis=0)


def head_cols(h, offset=0):
    return slice(offset + h * HD, offset + (h + 1) * HD)


def scores_of(q_ref, kv_refs, bias):
    return [
        lax.dot_general(
            jnp.concatenate([r[:, head_cols(h)] for r in kv_refs], axis=0),
            q_ref[:, head_cols(h)],
            (((1,), (1,)), ((), ())),
            preferred_element_type=F32,
        )
        + bias
        for h in range(q_ref.shape[1] // HD)
    ]


def raised_from(scores, peaks):
    return [jnp.exp((s - peaks[h : h + 1]) * HD ** (-0.5)) for h, s in enumerate(scores)]


def reduced(reduce, per_head):
    return jnp.concatenate([reduce(x, axis=0, keepdims=True) for x in per_head], axis=0)


def mixes_of(kv_refs, raised):
    inner = kv_refs[0].shape[1] // 2
    return [
        lax.dot_general(
            jnp.concatenate([r[:, head_cols(h, inner)] for r in kv_refs], axis=0),
            x.astype(BF16),
            (((0,), (0,)), ((), ())),
            preferred_element_type=F32,
        )
        for h, x in enumerate(raised)
    ]


def near_kernel(n_kv, tile_len, slots_of, lists_ref, q_weight_ref, _, normed_ref, *refs):
    kv_refs = refs[:n_kv]
    q_ref, peak_ref, total_ref, mix_ref = refs[n_kv:]
    q_ref[...] = projected(normed_ref[...], q_weight_ref[...])
    count, key_count = normed_ref.shape[0], sum(r.shape[0] for r in kv_refs)
    bias = masking(lists_ref, slots_of(), tile_len, 0, key_count, count)
    scores = scores_of(q_ref, kv_refs, bias)
    peaks = reduced(jnp.max, scores)
    raised = raised_from(scores, peaks)
    peak_ref[...] = peaks
    total_ref[...] = reduced(jnp.sum, raised)
    for h, mix in enumerate(mixes_of(kv_refs, raised)):
        mix_ref[head_cols(h), :] = mix


def finish_kernel(
    n_far, n_kv, tile_len, slots_of, has_far, first,
    lists_ref, modulate_ref, out_weight_ref, rows_ref, q_ref, peak_ref, total_ref, mix_ref, *refs
):
    mixed_ref, finished_ref = refs[n_kv:]

    def join(kv_refs, first):
        key_count = sum(r.shape[0] for r in kv_refs)
        bias = masking(lists_ref, slots_of(), tile_len, first, key_count, rows_ref.shape[0])
        scores = scores_of(q_ref, kv_refs, bias)
        before = peak_ref[...]
        peaks = jnp.maximum(reduced(jnp.max, scores), before)
        raised = raised_from(scores, peaks)
        kept = jnp.exp((before - peaks) * HD ** (-0.5))
        share = 1.0 / (total_ref[...] * kept + reduced(jnp.sum, raised))
        kept = kept * share
        for h, mix in enumerate(mixes_of(kv_refs, raised)):
            mixed_ref[head_cols(h), :] = (
                mix_ref[head_cols(h), :] * kept[h : h + 1] + mix * share[h : h + 1]
            ).astype(BF16)

    if n_far:
        far = has_far()

        @pl.when(far)
        def _():
            join(refs[:n_kv], first)

        @pl.when(jnp.logical_not(far))
        def _():
            join(refs[n_far:n_kv], first + sum(r.shape[0] for r in refs[:n_far]))

    else:
        join(refs[:n_kv], first)
    output_columns(0, mixed_ref, modulate_ref, out_weight_ref, rows_ref, finished_ref)


def output_columns(first, mixed_ref, modulate_ref, out_weight_ref, rows_ref, finished_ref):
    cols = slice(first, first + finished_ref.shape[1])
    branch = lax.dot_general(
        mixed_ref[...],
        out_weight_ref[:, cols],
        (((0,), (0,)), ((), ())),
        preferred_element_type=F32,
    )
    finished_ref[...] = (
        rows_ref[:, cols].astype(F32) + modulate_ref[2:3, cols] * branch
    ).astype(BF16)


def first_kernel(part_ref, whole_hbm, sem):
    copy = pltpu.make_async_copy(part_ref, whole_hbm.at[:, pl.ds(0, part_ref.shape[1])], sem)
    copy.start()
    copy.wait()


def rest_kernel(first, _, part_ref, whole_hbm, sem):
    copy = pltpu.make_async_copy(part_ref, whole_hbm.at[:, pl.ds(first, part_ref.shape[1])], sem)
    copy.start()
    copy.wait()


def swap_perm(size):
    return [(i, i ^ 1) for i in range(size)]


def relay_perm(size):
    return [(i, i + 2) for i in range(0, size - 2, 2)] + [(i, i - 2) for i in range(3, size, 2)]


def beyond_perm(size):
    return [((i + (2 if i % 2 == 0 else -2)) % size, i) for i in range(size)]


def in_hbm(x):
    return pltpu.with_memory_space_constraint(x, pltpu.HBM)


def after(x, *others):
    return lax.optimization_barrier((x, *others))[0]


def call(kernel, ins, outs, args, scratch=(), name=None, weight=1):
    return pl.pallas_call(
        kernel,
        out_shape=outs,
        in_specs=ins,
        out_specs=[VMEM] * len(outs),
        scratch_shapes=scratch,
        compiler_params=PARAMS,
        cost_estimate=pl.CostEstimate(flops=weight, bytes_accessed=0, transcendentals=0),
        name=name,
    )(*args)


def body(clip_tokens, qkv_weight, out_weight, modulation, domain_ids, tile_lists):
    col_tiles, tile_len, width = clip_tokens.shape[3:]
    own_count = col_tiles * tile_len
    inner = out_weight.shape[1]
    heads = inner // HD
    frames, rows = lax.axis_size("frame"), lax.axis_size("row")
    segments = lax.axis_size("segment")
    modulation_table = jnp.transpose(modulation[0], (1, 0, 2))
    weight = qkv_weight[0]
    own = clip_tokens.reshape(own_count, width)

    def held(count, wide, dtype=BF16):
        return pltpu.VMEM((count, wide), dtype)

    def from_partner(x):
        return lax.ppermute(x, "frame", swap_perm(frames))

    def from_beyond(x):
        return lax.ppermute(x, "frame", beyond_perm(frames))

    tokens = from_partner(own)
    lists = from_partner(tile_lists[0, 0])
    far = frames > 2
    sent = own_count * RAW // 8
    beyond = [from_beyond(own[:sent])] if far else []

    modulate, q_weight, pair_weight, kv_own, *tail = call(
        functools.partial(load_kernel, inner),
        [pl.BlockSpec(memory_space=pl.ANY)] + [HBM] * 3,
        [held(3, width, F32), held(width, inner), held(width, 2 * inner), held(own_count, 2 * inner)]
        + [held(own_count - sent, 2 * inner)] * far,
        [domain_ids, *map(in_hbm, (modulation_table, weight, own))],
        [
            pltpu.SMEM(domain_ids.shape, jnp.int32),
            pltpu.VMEM(modulation_table.shape, BF16),
            pltpu.VMEM((own_count, width), BF16),
            pltpu.SemaphoreType.DMA((4 + LOADS,)),
        ],
        "own_pairs",
    )
    kv_tail = [from_beyond(t) for t in tail]
    kv_beyond = [
        call(
            beyond_kernel,
            [VMEM] * 3,
            [held(sent, 2 * inner)],
            [modulate, pair_weight, b],
            name="beyond_pairs",
        )[0]
        for b in beyond
    ]
    near_tiles = 2 + far

    def slots_of():
        odd_frame = 1 - lax.axis_index("frame") % 2
        odd_row = lax.axis_index("row") % 2
        return [
            0,
            2 - odd_frame,
            1 + odd_frame,
            near_tiles + 1 - odd_row,
            near_tiles + odd_row,
        ]

    tokens = after(tokens, kv_own, *kv_beyond)
    kv_tokens, normed = call(
        pair_kernel,
        [VMEM] * 3,
        [held(own_count, 2 * inner), held(own_count, width)],
        [modulate, pair_weight, tokens],
        name="pairs",
    )
    kv_rows = [lax.ppermute(kv_tokens, "row", swap_perm(rows))]
    if rows > 2:
        kv_rows.append(lax.ppermute(kv_rows[0], "row", relay_perm(rows)))
    near = [kv_tokens, kv_own]
    q, *partial = call(
        functools.partial(near_kernel, len(near), tile_len, slots_of),
        [VMEM] * (4 + len(near)),
        [
            held(own_count, inner),
            held(heads, own_count, F32),
            held(heads, own_count, F32),
            held(inner, own_count, F32),
        ],
        [lists, q_weight, out_weight[0], normed, *near],
        name="near_attention",
        weight=10**10,
    )
    def has_far():
        frame = lax.axis_index("frame")
        return jnp.where(frame % 2 == 0, frame + 2 < frames, frame >= 2)

    late = [*kv_beyond, *kv_tail, *kv_rows]
    cuts = [width * sum(PARTS[:i]) // sum(PARTS) for i in range(len(PARTS) + 1)]
    mixed, *finished = call(
        functools.partial(
            finish_kernel,
            len(late) - len(kv_rows),
            len(late),
            tile_len,
            slots_of,
            has_far,
            sum(x.shape[0] for x in near),
        ),
        [VMEM] * (8 + len(late)),
        [held(inner, own_count), held(own_count, cuts[1])],
        [lists, modulate, out_weight[0], tokens, q, *partial, *late],
        name="finish",
    )
    for start, end in zip(cuts[1:-1], cuts[2:]):
        finished += call(
            functools.partial(output_columns, start),
            [VMEM] * 4,
            [held(own_count, end - start)],
            [mixed, modulate, out_weight[0], tokens],
            name="finish_rest",
        )
    onward = [
        (s * frames + f, (s + 1) % segments * frames + (f ^ 1))
        for s in range(segments)
        for f in range(frames)
    ]
    handed = [lax.ppermute(x, ("segment", "frame"), onward) for x in finished]
    result = jax.ShapeDtypeStruct((own_count, width), BF16)
    out = pl.pallas_call(
        first_kernel,
        out_shape=result,
        in_specs=[VMEM],
        out_specs=HBM,
        scratch_shapes=[pltpu.SemaphoreType.DMA],
        compiler_params=PARAMS,
        name="first_columns",
    )(handed[0])
    for start, part in zip(cuts[1:], handed[1:]):
        out = pl.pallas_call(
            functools.partial(rest_kernel, start),
            out_shape=result,
            in_specs=[HBM, VMEM],
            out_specs=HBM,
            scratch_shapes=[pltpu.SemaphoreType.DMA],
            input_output_aliases={0: 0},
            compiler_params=PARAMS,
            name="other_columns",
        )(out, part)
    return out.reshape(clip_tokens.shape)


def solution(mesh):
    return jax.shard_map(
        body,
        mesh=mesh,
        in_specs=(
            P("segment", "frame", "row", None, None, None),
            P("segment", None, None),
            P("segment", None, None),
            P("segment", None, None, None),
            P("segment"),
            P("frame", "row", None, None),
        ),
        out_specs=P("segment", "frame", "row", None, None, None),
        check_vma=False,
    )
```

```python
import functools

import jax
import jax.numpy as jnp
from jax import lax
from jax.experimental import pallas as pl
from jax.experimental.pallas import tpu as pltpu
from jax.sharding import PartitionSpec as P

HD = 128
EPSILON = 1e-06
MASKED = -1e30
RAW = 5
LOADS = 4
PARTS = (5, 4, 3)
F32 = jnp.float32
BF16 = jnp.bfloat16
VMEM = pl.BlockSpec(memory_space=pltpu.VMEM)
SMEM = pl.BlockSpec(memory_space=pltpu.SMEM)
HBM = pl.BlockSpec(memory_space=pltpu.HBM)
PARAMS = pltpu.CompilerParams(vmem_limit_bytes=32 * 1024 * 1024)


def modulate_rows(domain_ref, modulation_ref):
    table = modulation_ref[...].astype(F32)
    row = lax.broadcasted_iota(jnp.int32, table.shape, 1)
    return jnp.sum(jnp.where(row == domain_ref[0], table, 0.0), axis=1)


def normalize(rows, shift, scale):
    values = rows.astype(F32)
    centered = values - jnp.mean(values, axis=-1, keepdims=True)
    row_var = jnp.mean(centered * centered, axis=-1, keepdims=True)
    return (centered * lax.rsqrt(row_var + EPSILON) * (1.0 + scale) + shift).astype(BF16)


def normalized(refs, modulate_ref):
    shift, scale = modulate_ref[0:1, :], modulate_ref[1:2, :]
    return jnp.concatenate([normalize(r[...], shift, scale) for r in refs], axis=0)


def projected(rows, weight):
    return jnp.dot(rows, weight, preferred_element_type=F32).astype(BF16)


def load_kernel(
    inner, domain_hbm, modulation_hbm, weight_hbm, own_hbm,
    modulate_ref, q_weight_ref, weight_ref, kv_ref, *refs
):
    *tail_ref, domain_ref, modulation_ref, own_ref, sems = refs
    first = [
        pltpu.make_async_copy(domain_hbm, domain_ref, sems.at[0]),
        pltpu.make_async_copy(modulation_hbm, modulation_ref, sems.at[1]),
        pltpu.make_async_copy(own_hbm, own_ref, sems.at[2]),
    ]
    part = 2 * inner // LOADS
    loads = [
        pltpu.make_async_copy(
            weight_hbm.at[:, pl.ds(inner + i * part, part)],
            weight_ref.at[:, pl.ds(i * part, part)],
            sems.at[3 + i],
        )
        for i in range(LOADS)
    ]
    query = pltpu.make_async_copy(weight_hbm.at[:, pl.ds(0, inner)], q_weight_ref, sems.at[3 + LOADS])
    for load in first + loads + [query]:
        load.start()
    for load in first:
        load.wait()
    modulate_ref[...] = modulate_rows(domain_ref, modulation_ref)
    rows = normalized((own_ref,), modulate_ref)
    for i, load in enumerate(loads):
        load.wait()
        cols = slice(i * part, (i + 1) * part)
        pairs = projected(rows, weight_ref[:, cols])
        kv_ref[:, cols] = pairs
        for ref in tail_ref:
            ref[:, cols] = pairs[rows.shape[0] - ref.shape[0] :]
    query.wait()


def beyond_kernel(modulate_ref, weight_ref, rows_ref, kv_ref):
    kv_ref[...] = projected(normalized((rows_ref,), modulate_ref), weight_ref[...])


def pair_kernel(modulate_ref, weight_ref, rows_ref, kv_ref, normed_ref):
    rows = normalized((rows_ref,), modulate_ref)
    normed_ref[...] = rows
    kv_ref[...] = projected(rows, weight_ref[...])


def masking(lists_ref, slots, tile_len, first, key_count, query_count):
    col_tiles = query_count // tile_len
    numbers = lists_ref[...]
    slot = jnp.full(numbers.shape, slots[0], jnp.int32)
    for d in range(1, 5):
        slot = jnp.where(numbers // col_tiles == d, slots[d], slot)
    bits = jnp.sum(
        jnp.int32(1) << (slot * col_tiles + numbers % col_tiles), axis=1, keepdims=True
    )
    tile = lax.broadcasted_iota(jnp.int32, (1, query_count), 1) // tile_len
    row = jnp.zeros((1, query_count), jnp.int32)
    for t in range(col_tiles):
        row = jnp.where(tile == t, bits[t : t + 1, :], row)
    parts, end = [], first + key_count
    for p in range(first // tile_len, pl.cdiv(end, tile_len)):
        size = min(end, (p + 1) * tile_len) - max(first, p * tile_len)
        added = jnp.where((row >> p) & 1 == 1, 0.0, MASKED)
        parts.append(jnp.broadcast_to(added, (size, query_count)))
    return jnp.concatenate(parts, axis=0)


def head_cols(h, offset=0):
    return slice(offset + h * HD, offset + (h + 1) * HD)


def scores_of(q_ref, kv_refs, bias):
    return [
        lax.dot_general(
            jnp.concatenate([r[:, head_cols(h)] for r in kv_refs], axis=0),
            q_ref[:, head_cols(h)],
            (((1,), (1,)), ((), ())),
            preferred_element_type=F32,
        )
        + bias
        for h in range(q_ref.shape[1] // HD)
    ]


def raised_from(scores, peaks):
    return [jnp.exp((s - peaks[h : h + 1]) * HD ** (-0.5)) for h, s in enumerate(scores)]


def reduced(reduce, per_head):
    return jnp.concatenate([reduce(x, axis=0, keepdims=True) for x in per_head], axis=0)


def mixes_of(kv_refs, raised):
    inner = kv_refs[0].shape[1] // 2
    return [
        lax.dot_general(
            jnp.concatenate([r[:, head_cols(h, inner)] for r in kv_refs], axis=0),
            x.astype(BF16),
            (((0,), (0,)), ((), ())),
            preferred_element_type=F32,
        )
        for h, x in enumerate(raised)
    ]


def near_kernel(n_kv, tile_len, slots_of, lists_ref, q_weight_ref, _, normed_ref, *refs):
    kv_refs = refs[:n_kv]
    q_ref, peak_ref, total_ref, mix_ref = refs[n_kv:]
    q_ref[...] = projected(normed_ref[...], q_weight_ref[...])
    count, key_count = normed_ref.shape[0], sum(r.shape[0] for r in kv_refs)
    bias = masking(lists_ref, slots_of(), tile_len, 0, key_count, count)
    scores = scores_of(q_ref, kv_refs, bias)
    peaks = reduced(jnp.max, scores)
    raised = raised_from(scores, peaks)
    peak_ref[...] = peaks
    total_ref[...] = reduced(jnp.sum, raised)
    for h, mix in enumerate(mixes_of(kv_refs, raised)):
        mix_ref[head_cols(h), :] = mix


def finish_kernel(
    n_far, n_kv, tile_len, slots_of, has_far, first,
    lists_ref, modulate_ref, out_weight_ref, rows_ref, q_ref, peak_ref, total_ref, mix_ref, *refs
):
    mixed_ref, finished_ref = refs[n_kv:]

    def join(kv_refs, first):
        key_count = sum(r.shape[0] for r in kv_refs)
        bias = masking(lists_ref, slots_of(), tile_len, first, key_count, rows_ref.shape[0])
        scores = scores_of(q_ref, kv_refs, bias)
        before = peak_ref[...]
        peaks = jnp.maximum(reduced(jnp.max, scores), before)
        raised = raised_from(scores, peaks)
        kept = jnp.exp((before - peaks) * HD ** (-0.5))
        share = 1.0 / (total_ref[...] * kept + reduced(jnp.sum, raised))
        kept = kept * share
        for h, mix in enumerate(mixes_of(kv_refs, raised)):
            mixed_ref[head_cols(h), :] = (
                mix_ref[head_cols(h), :] * kept[h : h + 1] + mix * share[h : h + 1]
            ).astype(BF16)

    if n_far:
        far = has_far()

        @pl.when(far)
        def _():
            join(refs[:n_kv], first)

        @pl.when(jnp.logical_not(far))
        def _():
            join(refs[n_far:n_kv], first + sum(r.shape[0] for r in refs[:n_far]))

    else:
        join(refs[:n_kv], first)
    output_columns(0, mixed_ref, modulate_ref, out_weight_ref, rows_ref, finished_ref)


def output_columns(first, mixed_ref, modulate_ref, out_weight_ref, rows_ref, finished_ref):
    cols = slice(first, first + finished_ref.shape[1])
    branch = lax.dot_general(
        mixed_ref[...],
        out_weight_ref[:, cols],
        (((0,), (0,)), ((), ())),
        preferred_element_type=F32,
    )
    finished_ref[...] = (
        rows_ref[:, cols].astype(F32) + modulate_ref[2:3, cols] * branch
    ).astype(BF16)


def first_kernel(part_ref, whole_hbm, sem):
    copy = pltpu.make_async_copy(part_ref, whole_hbm.at[:, pl.ds(0, part_ref.shape[1])], sem)
    copy.start()
    copy.wait()


def rest_kernel(first, _, part_ref, whole_hbm, sem):
    copy = pltpu.make_async_copy(part_ref, whole_hbm.at[:, pl.ds(first, part_ref.shape[1])], sem)
    copy.start()
    copy.wait()


def swap_perm(size):
    return [(i, i ^ 1) for i in range(size)]


def relay_perm(size):
    return [(i, i + 2) for i in range(0, size - 2, 2)] + [(i, i - 2) for i in range(3, size, 2)]


def beyond_perm(size):
    return [((i + (2 if i % 2 == 0 else -2)) % size, i) for i in range(size)]


def in_hbm(x):
    return pltpu.with_memory_space_constraint(x, pltpu.HBM)


def after(x, *others):
    return lax.optimization_barrier((x, *others))[0]


def call(kernel, ins, outs, args, scratch=(), name=None, weight=1):
    return pl.pallas_call(
        kernel,
        out_shape=outs,
        in_specs=ins,
        out_specs=[VMEM] * len(outs),
        scratch_shapes=scratch,
        compiler_params=PARAMS,
        cost_estimate=pl.CostEstimate(flops=weight, bytes_accessed=0, transcendentals=0),
        name=name,
    )(*args)


def body(clip_tokens, qkv_weight, out_weight, modulation, domain_ids, tile_lists):
    col_tiles, tile_len, width = clip_tokens.shape[3:]
    own_count = col_tiles * tile_len
    inner = out_weight.shape[1]
    heads = inner // HD
    frames, rows = lax.axis_size("frame"), lax.axis_size("row")
    segments = lax.axis_size("segment")
    modulation_table = jnp.transpose(modulation[0], (1, 0, 2))
    weight = qkv_weight[0]
    own = clip_tokens.reshape(own_count, width)

    def held(count, wide, dtype=BF16):
        return pltpu.VMEM((count, wide), dtype)

    def from_partner(x):
        return lax.ppermute(x, "frame", swap_perm(frames))

    def from_beyond(x):
        return lax.ppermute(x, "frame", beyond_perm(frames))

    tokens = from_partner(own)

    far = frames > 2
    sent = own_count * RAW // 8
    beyond = [from_beyond(own[:sent])] if far else []

    modulate, q_weight, pair_weight, kv_own, *tail = call(
        functools.partial(load_kernel, inner),
        [pl.BlockSpec(memory_space=pl.ANY)] + [HBM] * 3,
        [held(3, width, F32), held(width, inner), held(width, 2 * inner), held(own_count, 2 * inner)]
        + [held(own_count - sent, 2 * inner)] * far,
        [domain_ids, *map(in_hbm, (modulation_table, weight, own))],
        [
            pltpu.SMEM(domain_ids.shape, jnp.int32),
            pltpu.VMEM(modulation_table.shape, BF16),
            pltpu.VMEM((own_count, width), BF16),
            pltpu.SemaphoreType.DMA((4 + LOADS,)),
        ],
        "own_pairs",
    )
    kv_tail = [from_beyond(t) for t in tail]
    kv_beyond = [
        call(
            beyond_kernel,
            [VMEM] * 3,
            [held(sent, 2 * inner)],
            [modulate, pair_weight, b],
            name="beyond_pairs",
        )[0]
        for b in beyond
    ]
    lists = from_partner(after(tile_lists[0, 0], kv_own))
    near_tiles = 2 + far

    def slots_of():
        odd_frame = 1 - lax.axis_index("frame") % 2
        odd_row = lax.axis_index("row") % 2
        return [
            0,
            2 - odd_frame,
            1 + odd_frame,
            near_tiles + 1 - odd_row,
            near_tiles + odd_row,
        ]

    tokens = after(tokens, kv_own, *kv_beyond)
    kv_tokens, normed = call(
        pair_kernel,
        [VMEM] * 3,
        [held(own_count, 2 * inner), held(own_count, width)],
        [modulate, pair_weight, tokens],
        name="pairs",
    )
    kv_rows = [lax.ppermute(kv_tokens, "row", swap_perm(rows))]
    if rows > 2:
        kv_rows.append(lax.ppermute(kv_rows[0], "row", relay_perm(rows)))
    near = [kv_tokens, kv_own]
    q, *partial = call(
        functools.partial(near_kernel, len(near), tile_len, slots_of),
        [VMEM] * (4 + len(near)),
        [
            held(own_count, inner),
            held(heads, own_count, F32),
            held(heads, own_count, F32),
            held(inner, own_count, F32),
        ],
        [lists, q_weight, out_weight[0], normed, *near],
        name="near_attention",
        weight=10**10,
    )
    def has_far():
        frame = lax.axis_index("frame")
        return jnp.where(frame % 2 == 0, frame + 2 < frames, frame >= 2)

    late = [*kv_beyond, *kv_tail, *kv_rows]
    cuts = [width * sum(PARTS[:i]) // sum(PARTS) for i in range(len(PARTS) + 1)]
    mixed, *finished = call(
        functools.partial(
            finish_kernel,
            len(late) - len(kv_rows),
            len(late),
            tile_len,
            slots_of,
            has_far,
            sum(x.shape[0] for x in near),
        ),
        [VMEM] * (8 + len(late)),
        [held(inner, own_count), held(own_count, cuts[1])],
        [lists, modulate, out_weight[0], tokens, q, *partial, *late],
        name="finish",
    )
    for start, end in zip(cuts[1:-1], cuts[2:]):
        finished += call(
            functools.partial(output_columns, start),
            [VMEM] * 4,
            [held(own_count, end - start)],
            [mixed, modulate, out_weight[0], tokens],
            name="finish_rest",
        )
    onward = [
        (s * frames + f, (s + 1) % segments * frames + (f ^ 1))
        for s in range(segments)
        for f in range(frames)
    ]
    handed = [lax.ppermute(x, ("segment", "frame"), onward) for x in finished]
    result = jax.ShapeDtypeStruct((own_count, width), BF16)
    out = pl.pallas_call(
        first_kernel,
        out_shape=result,
        in_specs=[VMEM],
        out_specs=HBM,
        scratch_shapes=[pltpu.SemaphoreType.DMA],
        compiler_params=PARAMS,
        name="first_columns",
    )(handed[0])
    for start, part in zip(cuts[1:], handed[1:]):
        out = pl.pallas_call(
            functools.partial(rest_kernel, start),
            out_shape=result,
            in_specs=[HBM, VMEM],
            out_specs=HBM,
            scratch_shapes=[pltpu.SemaphoreType.DMA],
            input_output_aliases={0: 0},
            compiler_params=PARAMS,
            name="other_columns",
        )(out, part)
    return out.reshape(clip_tokens.shape)


def solution(mesh):
    return jax.shard_map(
        body,
        mesh=mesh,
        in_specs=(
            P("segment", "frame", "row", None, None, None),
            P("segment", None, None),
            P("segment", None, None),
            P("segment", None, None, None),
            P("segment"),
            P("frame", "row", None, None),
        ),
        out_specs=P("segment", "frame", "row", None, None, None),
        check_vma=False,
    )
```

```python
import functools

import jax
import jax.numpy as jnp
from jax import lax
from jax.experimental import pallas as pl
from jax.experimental.pallas import tpu as pltpu
from jax.sharding import PartitionSpec as P

HD = 128
EPSILON = 1e-06
MASKED = -1e30
RAW = 5
LOADS = 4
PARTS = (6, 4, 2)
F32 = jnp.float32
BF16 = jnp.bfloat16
VMEM = pl.BlockSpec(memory_space=pltpu.VMEM)
SMEM = pl.BlockSpec(memory_space=pltpu.SMEM)
HBM = pl.BlockSpec(memory_space=pltpu.HBM)
PARAMS = pltpu.CompilerParams(vmem_limit_bytes=32 * 1024 * 1024)


def modulate_rows(domain_ref, modulation_ref):
    table = modulation_ref[...].astype(F32)
    row = lax.broadcasted_iota(jnp.int32, table.shape, 1)
    return jnp.sum(jnp.where(row == domain_ref[0], table, 0.0), axis=1)


def normalize(rows, shift, scale):
    values = rows.astype(F32)
    centered = values - jnp.mean(values, axis=-1, keepdims=True)
    row_var = jnp.mean(centered * centered, axis=-1, keepdims=True)
    return (centered * lax.rsqrt(row_var + EPSILON) * (1.0 + scale) + shift).astype(BF16)


def normalized(refs, modulate_ref):
    shift, scale = modulate_ref[0:1, :], modulate_ref[1:2, :]
    return jnp.concatenate([normalize(r[...], shift, scale) for r in refs], axis=0)


def projected(rows, weight):
    return jnp.dot(rows, weight, preferred_element_type=F32).astype(BF16)


def load_kernel(
    inner, domain_hbm, modulation_hbm, weight_hbm, own_hbm,
    modulate_ref, q_weight_ref, weight_ref, kv_ref, *refs
):
    *tail_ref, domain_ref, modulation_ref, own_ref, sems = refs
    first = [
        pltpu.make_async_copy(domain_hbm, domain_ref, sems.at[0]),
        pltpu.make_async_copy(modulation_hbm, modulation_ref, sems.at[1]),
        pltpu.make_async_copy(own_hbm, own_ref, sems.at[2]),
    ]
    part = 2 * inner // LOADS
    loads = [
        pltpu.make_async_copy(
            weight_hbm.at[:, pl.ds(inner + i * part, part)],
            weight_ref.at[:, pl.ds(i * part, part)],
            sems.at[3 + i],
        )
        for i in range(LOADS)
    ]
    query = pltpu.make_async_copy(weight_hbm.at[:, pl.ds(0, inner)], q_weight_ref, sems.at[3 + LOADS])
    for load in first + loads + [query]:
        load.start()
    for load in first:
        load.wait()
    modulate_ref[...] = modulate_rows(domain_ref, modulation_ref)
    rows = normalized((own_ref,), modulate_ref)
    for i, load in enumerate(loads):
        load.wait()
        cols = slice(i * part, (i + 1) * part)
        pairs = projected(rows, weight_ref[:, cols])
        kv_ref[:, cols] = pairs
        for ref in tail_ref:
            ref[:, cols] = pairs[rows.shape[0] - ref.shape[0] :]
    query.wait()


def beyond_kernel(modulate_ref, weight_ref, rows_ref, kv_ref):
    kv_ref[...] = projected(normalized((rows_ref,), modulate_ref), weight_ref[...])


def pair_kernel(modulate_ref, weight_ref, rows_ref, kv_ref, normed_ref):
    rows = normalized((rows_ref,), modulate_ref)
    normed_ref[...] = rows
    kv_ref[...] = projected(rows, weight_ref[...])


def masking(lists_ref, slots, tile_len, first, key_count, query_count):
    col_tiles = query_count // tile_len
    numbers = lists_ref[...]
    slot = jnp.full(numbers.shape, slots[0], jnp.int32)
    for d in range(1, 5):
        slot = jnp.where(numbers // col_tiles == d, slots[d], slot)
    bits = jnp.sum(
        jnp.int32(1) << (slot * col_tiles + numbers % col_tiles), axis=1, keepdims=True
    )
    tile = lax.broadcasted_iota(jnp.int32, (1, query_count), 1) // tile_len
    row = jnp.zeros((1, query_count), jnp.int32)
    for t in range(col_tiles):
        row = jnp.where(tile == t, bits[t : t + 1, :], row)
    parts, end = [], first + key_count
    for p in range(first // tile_len, pl.cdiv(end, tile_len)):
        size = min(end, (p + 1) * tile_len) - max(first, p * tile_len)
        added = jnp.where((row >> p) & 1 == 1, 0.0, MASKED)
        parts.append(jnp.broadcast_to(added, (size, query_count)))
    return jnp.concatenate(parts, axis=0)


def head_cols(h, offset=0):
    return slice(offset + h * HD, offset + (h + 1) * HD)


def scores_of(q_ref, kv_refs, bias):
    return [
        lax.dot_general(
            jnp.concatenate([r[:, head_cols(h)] for r in kv_refs], axis=0),
            q_ref[:, head_cols(h)],
            (((1,), (1,)), ((), ())),
            preferred_element_type=F32,
        )
        + bias
        for h in range(q_ref.shape[1] // HD)
    ]


def raised_from(scores, peaks):
    return [jnp.exp((s - peaks[h : h + 1]) * HD ** (-0.5)) for h, s in enumerate(scores)]


def reduced(reduce, per_head):
    return jnp.concatenate([reduce(x, axis=0, keepdims=True) for x in per_head], axis=0)


def mixes_of(kv_refs, raised):
    inner = kv_refs[0].shape[1] // 2
    return [
        lax.dot_general(
            jnp.concatenate([r[:, head_cols(h, inner)] for r in kv_refs], axis=0),
            x.astype(BF16),
            (((0,), (0,)), ((), ())),
            preferred_element_type=F32,
        )
        for h, x in enumerate(raised)
    ]


def near_kernel(n_kv, tile_len, slots_of, lists_ref, q_weight_ref, _, normed_ref, *refs):
    kv_refs = refs[:n_kv]
    q_ref, peak_ref, total_ref, mix_ref = refs[n_kv:]
    q_ref[...] = projected(normed_ref[...], q_weight_ref[...])
    count, key_count = normed_ref.shape[0], sum(r.shape[0] for r in kv_refs)
    bias = masking(lists_ref, slots_of(), tile_len, 0, key_count, count)
    scores = scores_of(q_ref, kv_refs, bias)
    peaks = reduced(jnp.max, scores)
    raised = raised_from(scores, peaks)
    peak_ref[...] = peaks
    total_ref[...] = reduced(jnp.sum, raised)
    for h, mix in enumerate(mixes_of(kv_refs, raised)):
        mix_ref[head_cols(h), :] = mix


def finish_kernel(
    n_far, n_kv, tile_len, slots_of, has_far, first,
    lists_ref, modulate_ref, out_weight_ref, rows_ref, q_ref, peak_ref, total_ref, mix_ref, *refs
):
    mixed_ref, finished_ref = refs[n_kv:]

    def join(kv_refs, first):
        key_count = sum(r.shape[0] for r in kv_refs)
        bias = masking(lists_ref, slots_of(), tile_len, first, key_count, rows_ref.shape[0])
        scores = scores_of(q_ref, kv_refs, bias)
        before = peak_ref[...]
        peaks = jnp.maximum(reduced(jnp.max, scores), before)
        raised = raised_from(scores, peaks)
        kept = jnp.exp((before - peaks) * HD ** (-0.5))
        share = 1.0 / (total_ref[...] * kept + reduced(jnp.sum, raised))
        kept = kept * share
        for h, mix in enumerate(mixes_of(kv_refs, raised)):
            mixed_ref[head_cols(h), :] = (
                mix_ref[head_cols(h), :] * kept[h : h + 1] + mix * share[h : h + 1]
            ).astype(BF16)

    if n_far:
        far = has_far()

        @pl.when(far)
        def _():
            join(refs[:n_kv], first)

        @pl.when(jnp.logical_not(far))
        def _():
            join(refs[n_far:n_kv], first + sum(r.shape[0] for r in refs[:n_far]))

    else:
        join(refs[:n_kv], first)
    output_columns(0, mixed_ref, modulate_ref, out_weight_ref, rows_ref, finished_ref)


def output_columns(first, mixed_ref, modulate_ref, out_weight_ref, rows_ref, finished_ref):
    cols = slice(first, first + finished_ref.shape[1])
    branch = lax.dot_general(
        mixed_ref[...],
        out_weight_ref[:, cols],
        (((0,), (0,)), ((), ())),
        preferred_element_type=F32,
    )
    finished_ref[...] = (
        rows_ref[:, cols].astype(F32) + modulate_ref[2:3, cols] * branch
    ).astype(BF16)


def first_kernel(part_ref, whole_hbm, sem):
    copy = pltpu.make_async_copy(part_ref, whole_hbm.at[:, pl.ds(0, part_ref.shape[1])], sem)
    copy.start()
    copy.wait()


def rest_kernel(first, _, part_ref, whole_hbm, sem):
    copy = pltpu.make_async_copy(part_ref, whole_hbm.at[:, pl.ds(first, part_ref.shape[1])], sem)
    copy.start()
    copy.wait()


def swap_perm(size):
    return [(i, i ^ 1) for i in range(size)]


def relay_perm(size):
    return [(i, i + 2) for i in range(0, size - 2, 2)] + [(i, i - 2) for i in range(3, size, 2)]


def beyond_perm(size):
    return [((i + (2 if i % 2 == 0 else -2)) % size, i) for i in range(size)]


def in_hbm(x):
    return pltpu.with_memory_space_constraint(x, pltpu.HBM)


def after(x, *others):
    return lax.optimization_barrier((x, *others))[0]


def call(kernel, ins, outs, args, scratch=(), name=None, weight=1):
    return pl.pallas_call(
        kernel,
        out_shape=outs,
        in_specs=ins,
        out_specs=[VMEM] * len(outs),
        scratch_shapes=scratch,
        compiler_params=PARAMS,
        cost_estimate=pl.CostEstimate(flops=weight, bytes_accessed=0, transcendentals=0),
        name=name,
    )(*args)


def body(clip_tokens, qkv_weight, out_weight, modulation, domain_ids, tile_lists):
    col_tiles, tile_len, width = clip_tokens.shape[3:]
    own_count = col_tiles * tile_len
    inner = out_weight.shape[1]
    heads = inner // HD
    frames, rows = lax.axis_size("frame"), lax.axis_size("row")
    segments = lax.axis_size("segment")
    modulation_table = jnp.transpose(modulation[0], (1, 0, 2))
    weight = qkv_weight[0]
    own = clip_tokens.reshape(own_count, width)

    def held(count, wide, dtype=BF16):
        return pltpu.VMEM((count, wide), dtype)

    def from_partner(x):
        return lax.ppermute(x, "frame", swap_perm(frames))

    def from_beyond(x):
        return lax.ppermute(x, "frame", beyond_perm(frames))

    tokens = from_partner(own)
    lists = from_partner(tile_lists[0, 0])
    far = frames > 2
    sent = own_count * RAW // 8
    beyond = [from_beyond(own[:sent])] if far else []

    modulate, q_weight, pair_weight, kv_own, *tail = call(
        functools.partial(load_kernel, inner),
        [pl.BlockSpec(memory_space=pl.ANY)] + [HBM] * 3,
        [held(3, width, F32), held(width, inner), held(width, 2 * inner), held(own_count, 2 * inner)]
        + [held(own_count - sent, 2 * inner)] * far,
        [domain_ids, *map(in_hbm, (modulation_table, weight, own))],
        [
            pltpu.SMEM(domain_ids.shape, jnp.int32),
            pltpu.VMEM(modulation_table.shape, BF16),
            pltpu.VMEM((own_count, width), BF16),
            pltpu.SemaphoreType.DMA((4 + LOADS,)),
        ],
        "own_pairs",
    )
    kv_tail = [from_beyond(t) for t in tail]
    kv_beyond = [
        call(
            beyond_kernel,
            [VMEM] * 3,
            [held(sent, 2 * inner)],
            [modulate, pair_weight, b],
            name="beyond_pairs",
        )[0]
        for b in beyond
    ]
    near_tiles = 2 + far

    def slots_of():
        odd_frame = 1 - lax.axis_index("frame") % 2
        odd_row = lax.axis_index("row") % 2
        return [
            0,
            2 - odd_frame,
            1 + odd_frame,
            near_tiles + 1 - odd_row,
            near_tiles + odd_row,
        ]

    tokens = after(tokens, kv_own, *kv_beyond)
    kv_tokens, normed = call(
        pair_kernel,
        [VMEM] * 3,
        [held(own_count, 2 * inner), held(own_count, width)],
        [modulate, pair_weight, tokens],
        name="pairs",
    )
    kv_rows = [lax.ppermute(kv_tokens, "row", swap_perm(rows))]
    if rows > 2:
        kv_rows.append(lax.ppermute(kv_rows[0], "row", relay_perm(rows)))
    near = [kv_tokens, kv_own]
    q, *partial = call(
        functools.partial(near_kernel, len(near), tile_len, slots_of),
        [VMEM] * (4 + len(near)),
        [
            held(own_count, inner),
            held(heads, own_count, F32),
            held(heads, own_count, F32),
            held(inner, own_count, F32),
        ],
        [lists, q_weight, out_weight[0], normed, *near],
        name="near_attention",
        weight=10**10,
    )
    def has_far():
        frame = lax.axis_index("frame")
        return jnp.where(frame % 2 == 0, frame + 2 < frames, frame >= 2)

    late = [*kv_beyond, *kv_tail, *kv_rows]
    cuts = [width * sum(PARTS[:i]) // sum(PARTS) for i in range(len(PARTS) + 1)]
    mixed, *finished = call(
        functools.partial(
            finish_kernel,
            len(late) - len(kv_rows),
            len(late),
            tile_len,
            slots_of,
            has_far,
            sum(x.shape[0] for x in near),
        ),
        [VMEM] * (8 + len(late)),
        [held(inner, own_count), held(own_count, cuts[1])],
        [lists, modulate, out_weight[0], tokens, q, *partial, *late],
        name="finish",
    )
    for start, end in zip(cuts[1:-1], cuts[2:]):
        finished += call(
            functools.partial(output_columns, start),
            [VMEM] * 4,
            [held(own_count, end - start)],
            [mixed, modulate, out_weight[0], tokens],
            name="finish_rest",
        )
    onward = [
        (s * frames + f, (s + 1) % segments * frames + (f ^ 1))
        for s in range(segments)
        for f in range(frames)
    ]
    handed = [lax.ppermute(x, ("segment", "frame"), onward) for x in finished]
    result = jax.ShapeDtypeStruct((own_count, width), BF16)
    out = pl.pallas_call(
        first_kernel,
        out_shape=result,
        in_specs=[VMEM],
        out_specs=HBM,
        scratch_shapes=[pltpu.SemaphoreType.DMA],
        compiler_params=PARAMS,
        name="first_columns",
    )(handed[0])
    for start, part in zip(cuts[1:], handed[1:]):
        out = pl.pallas_call(
            functools.partial(rest_kernel, start),
            out_shape=result,
            in_specs=[HBM, VMEM],
            out_specs=HBM,
            scratch_shapes=[pltpu.SemaphoreType.DMA],
            input_output_aliases={0: 0},
            compiler_params=PARAMS,
            name="other_columns",
        )(out, part)
    return out.reshape(clip_tokens.shape)


def solution(mesh):
    return jax.shard_map(
        body,
        mesh=mesh,
        in_specs=(
            P("segment", "frame", "row", None, None, None),
            P("segment", None, None),
            P("segment", None, None),
            P("segment", None, None, None),
            P("segment"),
            P("frame", "row", None, None),
        ),
        out_specs=P("segment", "frame", "row", None, None, None),
        check_vma=False,
    )
```
